512 devices in a mesh: head: 8 (over x, core), inner: 4 (over y_lo), outer: 16 (over y_hi, z).
Axes of the slice: x: 4, y: 8 (y_hi: 2, y_lo: 4; y = y_hi * 4 + y_lo), z: 8, core: 2. Of those that a mesh axis runs over, the one named last changes fastest.
Arguments:
- query: bfloat16 [8192, 4096], P(('outer', 'inner', 'head')), may hold values from -80 to 80
- key: bfloat16 [8192, 1024], P(('outer', 'inner', 'head')), may hold values from -6 to 6
- value: bfloat16 [8192, 1024], P(('outer', 'inner', 'head')), may hold values from -6 to 6
- doc_lengths: int32 [24], replicated, may hold values from 1 to 2048, 8192 in all
- resid: bfloat16 [8192, 4096], P('outer', 'inner'), may hold values from -20 to 20
- norm_gain: float32 [4096], P('inner'), may hold values from 0.1 to 1.9
- w_out: bfloat16 [4096, 4096], P('head', ('inner', 'outer')), may hold values from -0.09375 to 0.09375
- w_gate_up: bfloat16 [2, 4096, 7168], P(None, ('inner', 'outer'), 'head'), may hold values from -0.09375 to 0.09375
- w_down: bfloat16 [7168, 4096], P('head', ('inner', 'outer')), may hold values from -0.0625 to 0.0625
Outputs:
- context: bfloat16 [8192, 4096], P(('outer', 'inner'), 'head')
- layer_out: bfloat16 [8192, 4096], P(('outer', 'head'), 'inner')
The draws below stay inside these ranges and needn't reach their ends.
Inputs may be any that keep to these rules, and one draw needn't show every extreme that they name: `doc_lengths`: the 24 lengths sum to 8192, and the longest is exactly 2048.
All inputs are finite; a program needn't handle non-finite values.
Results may differ from the reference program's by a relative error of at most 0.03.
Values may be sent and summed in bfloat16 or wider, within the bound.
A program may use at most 64 MiB of HBM per device.

```python
import math
import jax
import jax.numpy as jnp
import numpy as np
from jax import lax

D = 4096
QUERY_HEADS = 32
KEY_VALUE_HEADS = 8
HEAD_WIDTH = 128
FF = 7168
SEQUENCE_BLOCK = 128
DOCS = 24
WINDOW_LENGTH = 8192
DOC_MOST = 2048
N_HEAD = 8
N_INNER = 4


def shared_keys(key):
    return jnp.clip(jax.random.normal(key, (WINDOW_LENGTH, KEY_VALUE_HEADS * HEAD_WIDTH), jnp.float32), -4.0, 4.0)


def draw_key(key, part):
    base_offset = shared_keys(key)
    return base_offset.astype(jnp.bfloat16)


def draw_query(key, part):
    key = jax.random.fold_in(key, 1)
    own_rows = jnp.clip(jax.random.normal(key, (WINDOW_LENGTH, QUERY_HEADS * HEAD_WIDTH), jnp.float32), -4.0, 4.0)
    return own_rows.astype(jnp.bfloat16)


def draw_resid(key, part):
    key = jax.random.fold_in(key, 3)
    noise_key, column_key, row_key = jax.random.split(key, 3)
    column_place = jnp.arange(D, dtype=jnp.float32)[None, :] / (D - 1)
    rough = jax.random.uniform(column_key, (1, D), jnp.float32, -0.5, 0.5)
    row_scale = jnp.exp(jax.random.uniform(row_key, (WINDOW_LENGTH, 1), jnp.float32, -1.6, 0.7))
    column_scale = jnp.exp(1.1 * (column_place - 1.0) + rough)
    field = jnp.clip(jax.random.normal(noise_key, (WINDOW_LENGTH, D), jnp.float32), -4.0, 4.0)
    return (field * column_scale * row_scale).astype(jnp.bfloat16)


def levels(stream_key, extent, cuts, low, top_value):
    level, own = 1.0, jax.random.fold_in(stream_key, 6)
    for position, shards_of in cuts:
        heights = jnp.exp(jax.random.uniform(jax.random.fold_in(own, position), (shards_of,), jnp.float32, low / len(cuts), top_value / len(cuts)))
        level = level * jnp.repeat(heights, extent[position] // shards_of).reshape([-1 if axis == position else 1 for axis in range(len(extent))])
    return level


def profile(number_of, total, limit, lean):
    weights = [(1 << 20) // math.isqrt(grade ** lean) + 1 for grade in range(2, number_of + 1)]
    surplus, counts = total - limit - (number_of - 1), [1] * (number_of - 1)
    while surplus > 0:
        free = [i for i in range(number_of - 1) if counts[i] < limit]
        mass, left = sum([weights[i] for i in free]), surplus
        for i in free:
            extra = min(limit - counts[i], max(1, left * weights[i] // mass), surplus)
            counts[i] = counts[i] + extra
            surplus = surplus - extra
    return np.array([limit] + counts)


def uneven(own_key, number_of, total, reach, lean):
    if number_of == 2:
        one = jax.random.randint(own_key, (), max(1, total - reach), min(reach, total - 1) + 1)
        return jnp.stack([one, total - one])
    tallies = jnp.asarray(profile(number_of, total, reach, lean), jnp.int32)
    pairs = (number_of - 1) // 2
    source_of, sink = tallies[1:1 + 2 * pairs:2], tallies[2:2 + 2 * pairs:2]
    room = jnp.minimum(source_of - 1, reach - sink)
    passed = jax.random.randint(jax.random.fold_in(own_key, 1), (pairs,), 0, 1 << 20) % (room + 1)
    tallies = tallies.at[1:1 + 2 * pairs:2].set(source_of - passed).at[2:2 + 2 * pairs:2].set(sink + passed)
    return tallies[jax.random.permutation(jax.random.fold_in(own_key, 2), number_of)]


def gaussian(own_key, extent, scale, most, cuts=(), kind=jnp.bfloat16):
    array = scale * jax.random.normal(own_key, extent, jnp.float32)
    if cuts:
        array = array * levels(own_key, extent, cuts, -0.22, 0.18)
    return jnp.clip(array, -most, most).astype(kind)


def setup_inputs(seed: int = 0) -> dict:
    streams_of = jax.random.split(jax.random.key(seed), 10)
    return {
        "query": draw_query(jax.random.fold_in(streams_of[9], 71), 0),
        "key": draw_key(jax.random.fold_in(streams_of[9], 71), 0),
        "value": gaussian(streams_of[2], (WINDOW_LENGTH, KEY_VALUE_HEADS * HEAD_WIDTH), 1.0, 6.0, ((0, 512),)),
        "doc_lengths": uneven(streams_of[3], DOCS, WINDOW_LENGTH, DOC_MOST, 2).astype(jnp.int32),
        "resid": draw_resid(jax.random.fold_in(streams_of[9], 71), 0),
        "norm_gain": jnp.clip(1.0 + 0.18 * jax.random.normal(streams_of[5], (D,), jnp.float32), 0.1, 1.9),
        "w_out": gaussian(streams_of[6], (QUERY_HEADS * HEAD_WIDTH, D), (QUERY_HEADS * HEAD_WIDTH) ** -0.5, 0.09375, ((0, 8), (1, 64))),
        "w_gate_up": gaussian(streams_of[7], (2, D, FF), D ** -0.5, 0.09375, ((1, 64), (2, 8))),
        "w_down": gaussian(streams_of[8], (FF, D), FF ** -0.5, 0.0625, ((0, 8), (1, 64))),
    }


def segment_ids(positions, doc_lengths):
    bounds = jnp.cumsum(doc_lengths).astype(jnp.int32)
    return lax.optimization_barrier(jnp.sum((bounds[None, :] <= positions[:, None]).astype(jnp.int32), axis=1)).astype(jnp.int32)

def rounded_back(values):
    return lax.optimization_barrier(values.astype(jnp.bfloat16)).astype(jnp.float32)

def reference(query, key, value, doc_lengths, resid, norm_gain, w_out, w_gate_up, w_down):
    group_width = QUERY_HEADS // KEY_VALUE_HEADS
    score_scale = HEAD_WIDTH ** (-0.5)
    positions = jnp.arange(WINDOW_LENGTH, dtype=jnp.int32)
    all_segments = segment_ids(positions, doc_lengths)
    expanded_keys = key.astype(jnp.float32).reshape(WINDOW_LENGTH, KEY_VALUE_HEADS, HEAD_WIDTH)
    expanded_values = value.astype(jnp.float32).reshape(WINDOW_LENGTH, KEY_VALUE_HEADS, HEAD_WIDTH)

    def query_block(block_index):
        anchor = (block_index * SEQUENCE_BLOCK).astype(jnp.int32)
        query_matrix = lax.dynamic_slice_in_dim(query, anchor, SEQUENCE_BLOCK, 0).astype(jnp.float32)
        query_matrix = query_matrix.reshape(SEQUENCE_BLOCK, KEY_VALUE_HEADS, group_width, HEAD_WIDTH)
        scores = jnp.einsum('qkgd,nkd->kgqn', query_matrix, expanded_keys) * score_scale
        query_place = anchor + jnp.arange(SEQUENCE_BLOCK, dtype=jnp.int32)
        query_segment = lax.dynamic_slice_in_dim(all_segments, anchor, SEQUENCE_BLOCK, 0)
        allowed = (positions[None, :] <= query_place[:, None]) & (all_segments[None, :] == query_segment[:, None])
        masked = jnp.where(allowed, scores, -1e+30)
        row_max = lax.optimization_barrier(jnp.max(masked, axis=-1, keepdims=True))
        exp_scores = jnp.where(allowed, jnp.exp(masked - row_max), 0.0)
        totals = lax.optimization_barrier(jnp.sum(exp_scores, axis=-1))
        summed = jnp.einsum('kgqn,nkd->kgqd', rounded_back(exp_scores), expanded_values)
        result = summed / totals[..., None]
        return jnp.transpose(result, (2, 0, 1, 3)).reshape(SEQUENCE_BLOCK, QUERY_HEADS * HEAD_WIDTH).astype(jnp.bfloat16)
    context = lax.map(query_block, jnp.arange(WINDOW_LENGTH // SEQUENCE_BLOCK, dtype=jnp.int32)).reshape(WINDOW_LENGTH, QUERY_HEADS * HEAD_WIDTH)
    head_cols = QUERY_HEADS * HEAD_WIDTH // N_HEAD
    projected = jnp.zeros((WINDOW_LENGTH, D), jnp.float32)
    for head_group in range(N_HEAD):
        lower = head_group * head_cols
        product = jnp.dot(context[:, lower:lower + head_cols], w_out[lower:lower + head_cols, :], preferred_element_type=jnp.float32)
        projected = projected + rounded_back(product)
    hidden_state = (resid.astype(jnp.float32) + projected).astype(jnp.bfloat16)
    state_wide = lax.optimization_barrier(hidden_state).astype(jnp.float32)
    mean_square = lax.optimization_barrier(jnp.mean(state_wide * state_wide, axis=1, keepdims=True))
    normed = (state_wide * lax.rsqrt(mean_square + 1e-05) * norm_gain[None, :]).astype(jnp.bfloat16)
    feature_cols = D // N_INNER
    gate_sum = jnp.zeros((WINDOW_LENGTH, FF), jnp.float32)
    up_sum = jnp.zeros((WINDOW_LENGTH, FF), jnp.float32)
    for inner_block in range(N_INNER):
        lower = inner_block * feature_cols
        normed_part = normed[:, lower:lower + feature_cols]
        gate_sum = gate_sum + rounded_back(jnp.dot(normed_part, w_gate_up[0, lower:lower + feature_cols, :], preferred_element_type=jnp.float32))
        up_sum = up_sum + rounded_back(jnp.dot(normed_part, w_gate_up[1, lower:lower + feature_cols, :], preferred_element_type=jnp.float32))
    activated = (jax.nn.silu(gate_sum) * up_sum).astype(jnp.bfloat16)
    hidden_cols = FF // N_HEAD
    down_sum = jnp.zeros((WINDOW_LENGTH, D), jnp.float32)
    for head_group in range(N_HEAD):
        lower = head_group * hidden_cols
        product = jnp.dot(activated[:, lower:lower + hidden_cols], w_down[lower:lower + hidden_cols, :], preferred_element_type=jnp.float32)
        down_sum = down_sum + rounded_back(product)
    layer_out = (state_wide + down_sum).astype(jnp.bfloat16)
    return (context, layer_out)
```

```python
import jax
import jax.numpy as jnp
from jax import lax
from jax.experimental import pallas as pl
from jax.experimental.pallas import tpu as pltpu
from jax.sharding import PartitionSpec as P

MESH = pl.DeviceIdType.MESH
D = 4096
BF = jnp.bfloat16
F32 = jnp.float32
SCALE = 128 ** (-0.5)
DOCS = 24
NX, NY, NZ = 4, 8, 8
BACK = 5


def nt(a, b):
    return lax.dot_general(a, b, (((1,), (1,)), ((), ())), preferred_element_type=F32)


def kernel(
    q_ref, k_ref, v_ref, docs_ref, resid_ref, gain_ref, wo_ref, wgu_ref, wd_ref,
    ctx_ref, out_ref,
    q_all, kv, scores, ctx_all, wo_all, w_all, res, gains,
    proj, proj_in, hid, acc, act, down, x_in, x_sum, y_in, ring_r, ring_l, odd_sum, odd_in,
    send_sem, recv_sem, local_sem,
):
    head = lax.axis_index("head")
    y_lo = lax.axis_index("inner")
    outer = lax.axis_index("outer")
    x, c = head // 2, head % 2
    y_hi, z = outer // NZ, outer % NZ
    y = y_hi * 4 + y_lo
    other = 1 - c

    def to_head(h):
        return {"head": h}

    def to_x(i):
        return {"head": i * 2 + c}

    def to_y(i):
        return {"inner": i % 4, "outer": (i // 4) * NZ + z}

    def to_z(i):
        return {"outer": y_hi * NZ + i}

    sibling = to_head(x * 2 + other)

    def feat(i):
        return (i % 4) * 2 + i // 4

    counter = [0]
    sends, locals_ = [], []

    def new(count=1):
        counter[0] += count
        return counter[0] - count

    def remote(src, dst, sid, dev):
        return pltpu.make_async_remote_copy(
            src_ref=src, dst_ref=dst, send_sem=send_sem.at[sid], recv_sem=recv_sem.at[sid],
            device_id=dev, device_id_type=MESH,
        )

    def push(src, dst, sid, dev):
        copy = remote(src, dst, sid, dev)
        copy.start()
        sends.append(copy)

    def arrive(dst, sid):
        remote(dst, dst, sid, sibling).wait_recv()

    local_count = [0]

    def local(src, dst):
        copy = pltpu.make_async_copy(src, dst, local_sem.at[local_count[0]])
        local_count[0] += 1
        copy.start()
        return copy

    def ring(n, me, to, chunk, half, arrived=None):
        steps = n // 2
        sr, sl = new(steps), new(steps)
        right, left = to((me + 1) % n), to((me + n - 1) % n)

        def run():
            for s in range(steps):
                back, ahead = (me - s + n) % n, (me + s) % n
                if s > 0:
                    arrive(chunk(back), sr + s - 1)
                    arrive(chunk(ahead), sl + s - 1)
                if s < steps - 1:
                    push(chunk(back), chunk(back), sr + s, right)
                    push(chunk(ahead), chunk(ahead), sl + s, left)
                else:
                    push(half(back, 0), half(back, 0), sr + s, right)
                    push(half(ahead, 1), half(ahead, 1), sl + s, left)
                if arrived is not None:
                    arrived(back, 2 * s)
                    if s > 0:
                        arrived(ahead, 2 * s - 1)
                yield
            far = (me + steps) % n
            arrive(half(far, 0), sr + steps - 1)
            arrive(half(far, 1), sl + steps - 1)
            if arrived is not None:
                arrived(far, 2 * steps - 1)

        return run()

    def finish(gen):
        for _ in gen:
            pass

    barrier = pltpu.get_barrier_semaphore()
    for k in range(1, 8):
        pl.semaphore_signal(barrier, inc=1, device_id=to_head((head + k) % 8), device_id_type=MESH)
        pl.semaphore_signal(barrier, inc=1, device_id=to_y((y + k) % NY), device_id_type=MESH)
        pl.semaphore_signal(barrier, inc=1, device_id=to_z((z + k) % NZ), device_id_type=MESH)
    pl.semaphore_wait(barrier, 21)

    kv_sid, q_sid = new(16), new(8)
    for k in range(1, 8):
        peer = (head + k) % 8
        cols = pl.ds(pl.multiple_of(peer * 128, 128), 128)
        push(k_ref.at[:, cols], kv.at[0, y, 0, head], kv_sid + k, to_head(peer))
        push(v_ref.at[:, cols], kv.at[0, y, 1, head], kv_sid + 8 + k, to_head(peer))
    own = pl.ds(pl.multiple_of(head * 128, 128), 128)
    kv[0, y, 0, head] = k_ref[:, own]
    kv[0, y, 1, head] = v_ref[:, own]
    for k in range(1, 8):
        peer = (head + k) % 8
        cols = pl.ds(pl.multiple_of(peer * 512, 512), 512)
        push(q_ref.at[:, cols], q_all.at[head], q_sid + k, to_head(peer))
    q_all[head] = q_ref[:, pl.ds(pl.multiple_of(head * 512, 512), 512)]

    for k in range(1, 8):
        peer = (head + 8 - k) % 8
        arrive(kv.at[0, y, 0, peer], kv_sid + k)
        arrive(kv.at[0, y, 1, peer], kv_sid + 8 + k)
    z_sid = new(BACK)
    for k in range(1, BACK):
        push(kv.at[0, y], kv.at[k, y], z_sid + k, to_z((z + k) % NZ))

    def lanes(core, width):
        return pl.ds(pl.multiple_of(core * width, width), width)

    def shared_ring(buf_chunk, buf_half):
        sid = new(8)
        gen = ring(
            NZ, z, to_z, lambda i: buf_chunk(i, c), lambda i, b: buf_half(i, b, c),
            lambda i, n: push(buf_chunk(i, c), buf_chunk(i, c), sid + n, sibling),
        )

        def wait_sibling():
            for n in range(8):
                step = (n + 1) // 2
                i = (z + step) % NZ if n % 2 else (z - step + NZ) % NZ
                arrive(buf_chunk(i, other), sid + n)

        return gen, wait_sibling

    wo_copy = local(wo_ref, wo_all.at[z, :, lanes(c, 512)])
    wo_ring, wo_wait = shared_ring(
        lambda i, s: wo_all.at[i, :, lanes(s, 512)],
        lambda i, b, s: wo_all.at[i, pl.ds(b * 32, 32), lanes(s, 512)],
    )

    res_rows = pl.ds(pl.multiple_of(head * 64, 64), 64)
    res_sid = new()
    push(
        resid_ref.at[res_rows, lanes(1 - y_hi, 512)], res.at[y_hi], res_sid,
        to_y((1 - y_hi) * 4 + y_lo),
    )
    res_copy = local(resid_ref.at[res_rows, lanes(y_hi, 512)], res.at[y_hi])
    gain_sid = new(4)
    for k in range(1, 4):
        push(gain_ref, gains.at[y_lo], gain_sid + k, to_y(y_hi * 4 + (y_lo + k) % 4))
    gains[y_lo] = gain_ref[...]

    kv_rings = [
        ring(
            NY, y, to_y,
            lambda i, dz=dz: kv.at[dz, i],
            lambda i, b, dz=dz: kv.at[dz, i, b],
        )
        for dz in range(BACK)
    ]
    for t in range(BACK + 4):
        for dz in range(BACK):
            if 0 <= t - dz <= 4:
                if t == dz and dz > 0:
                    arrive(kv.at[dz, y], z_sid + dz)
                next(kv_rings[dz], None)
        if t == 2:
            wo_copy.wait()
        if t >= 2:
            next(wo_ring, None)
    finish(wo_ring)

    w_sid = new(24)

    def w_cols(part, s):
        return pl.ds(pl.multiple_of(s * 384 + part * 128, 128), 128)

    def w_sources(i):
        cols = pl.ds(pl.multiple_of(i * 128, 128), 128)
        return wgu_ref.at[0, :, cols], wgu_ref.at[1, :, cols], wd_ref.at[:, cols]

    for k in range(1, NY):
        peer = (y + k) % NY

        @pl.when(peer != NY - 1)
        def _(k=k, peer=peer):
            for part, src in enumerate(w_sources(peer)):
                remote(
                    src, w_all.at[feat(y), z, :, w_cols(part, c)], w_sid + 3 * k + part, to_y(peer)
                ).start()

    @pl.when(y != NY - 1)
    def _():
        for part, src in enumerate(w_sources(y)):
            pltpu.make_async_copy(
                src, w_all.at[feat(y), z, :, w_cols(part, c)], local_sem.at[8 + part]
            ).start()

    @pl.when(y == NY - 1)
    def _():
        def zero(f, _):
            w_all[f, z, :, lanes(c, 384)] = jnp.zeros((64, 384), BF)
            return 0

        lax.fori_loop(0, 8, zero, 0)

    for k in range(1, 8):
        arrive(q_all.at[(head + 8 - k) % 8], q_sid + k)
    place = outer * 512 + y_lo * 128 + lax.broadcasted_iota(jnp.int32, (128, 1), 0)
    start = jnp.zeros((128, 1), jnp.int32)
    bound = jnp.int32(0)
    for j in range(DOCS):
        bound = bound + docs_ref[j]
        start = jnp.where(bound <= place, bound, start)
    for dz in range(BACK):
        half = jnp.where(z >= dz, y_hi, 1 - y_hi)
        keys = kv[dz, pl.ds(half * 4, 4), 0].reshape(512, 128)
        key_place = (outer - dz) * 512 + lax.broadcasted_iota(jnp.int32, (1, 512), 1)
        bias = jnp.where((key_place <= place) & (key_place >= start), 0.0, -1e30)
        for g in range(4):
            heads_q = q_all[:, :, g * 128:(g + 1) * 128].reshape(128, 128)
            scores[g, :, dz * 512:(dz + 1) * 512] = nt(heads_q, keys) * SCALE + bias
    for g in range(4):
        s = scores[g]
        e = jnp.exp(s - jnp.max(s, axis=1, keepdims=True))
        total = jnp.sum(e, axis=1, keepdims=True)
        e = e.astype(BF)
        summed = jnp.zeros((128, 128), F32)
        for dz in range(BACK):
            half = jnp.where(z >= dz, y_hi, 1 - y_hi)
            values = kv[dz, pl.ds(half * 4, 4), 1].reshape(512, 128)
            summed += jnp.dot(e[:, dz * 512:(dz + 1) * 512], values, preferred_element_type=F32)
        ctx_ref[:, g * 128:(g + 1) * 128] = (summed / total).astype(BF)

    def half_rows(i):
        return pl.ds(pl.multiple_of(i * 64, 64), 64)

    ctx_sid = new()
    push(ctx_ref.at[half_rows(other)], ctx_all.at[y, :, lanes(c, 512)], ctx_sid, sibling)
    ctx_all[y, :, lanes(c, 512)] = ctx_ref[half_rows(c), :]

    @pl.when(y != NY - 1)
    def _():
        for part, src in enumerate(w_sources(y)):
            pltpu.make_async_copy(
                src, w_all.at[feat(y), z, :, w_cols(part, c)], local_sem.at[8 + part]
            ).wait()
        for k in range(1, NY):
            for part in range(3):
                dst = w_all.at[feat((y + NY - k) % NY), z, :, w_cols(part, c)]
                arrive(dst, w_sid + 3 * k + part)

    w_ring, w_wait = shared_ring(
        lambda i, s: w_all.at[:, i, :, lanes(s, 384)],
        lambda i, b, s: w_all.at[pl.ds(b * 4, 4), i, :, lanes(s, 384)],
    )
    next(w_ring)
    arrive(ctx_all.at[y, :, lanes(other, 512)], ctx_sid)
    finish(ring(
        NY, y, to_y, lambda i: ctx_all.at[i], lambda i, b: ctx_all.at[i, pl.ds(b * 32, 32)]
    ))

    wo_wait()
    next(w_ring)

    def project(i, _):
        rows = ctx_all[pl.ds(i * 2, 2)].reshape(128, 1024)
        part = nt(rows, wo_all[...].reshape(512, 1024)).astype(BF).reshape(2, 64, 512)
        proj[i // 2, pl.ds((i % 2) * 2, 2)] = part
        return 0

    lax.fori_loop(0, 4, project, 0)
    proj_sid = new(4)
    for k in range(1, NX):
        peer = (x + k) % NX
        push(proj.at[:, peer], proj_in.at[k - 1], proj_sid + k, to_x(peer))
    res_copy.wait()
    arrive(res.at[1 - y_hi], res_sid)
    for k in range(1, NX):
        arrive(proj_in.at[k - 1], proj_sid + k)
    for g in range(2):
        total = proj[g, x].astype(F32)
        for k in range(3):
            total += proj_in[k, g].astype(F32)
        hid[feat(y), g, x] = (res[g].astype(F32) + total).astype(BF)

    first_sid, second_sid = new(4), new(32)

    def along_x(i, n):
        for k in range(1, NX):
            push(hid.at[feat(i), 1, x], hid.at[feat(i), 1, x], second_sid + 4 * n + k, to_x((x + k) % NX))

    for k in range(1, NX):
        push(hid.at[feat(y), 0, x], hid.at[feat(y), 0, x], first_sid + k, to_x((x + k) % NX))
    y_first = ring(
        NY, y, to_y, lambda i: hid.at[feat(i), 1, x],
        lambda i, b: hid.at[feat(i), 1, x, pl.ds(b * 32, 32)], along_x,
    )
    next(y_first)
    for k in range(1, NX):
        arrive(hid.at[feat(y), 0, (x + NX - k) % NX], first_sid + k)
    x_first = ring(
        NY, y, to_y, lambda i: hid.at[feat(i), 0],
        lambda i, b: hid.at[feat(i), 0, pl.ds(b * 2, 2)],
    )
    for s in range(4):
        next(x_first, None)
        next(y_first, None)
        if s in (0, 2):
            next(w_ring, None)
    finish(w_ring)
    finish(y_first)
    finish(x_first)
    for n in range(8):
        step = (n + 1) // 2
        i = (y + step) % NY if n % 2 else (y - step + NY) % NY
        for k in range(1, NX):
            arrive(hid.at[feat(i), 1, (x + NX - k) % NX], second_sid + 4 * n + k)
    for k in range(1, 4):
        arrive(gains.at[(y_lo + 4 - k) % 4], gain_sid + k)
    w_wait()

    acc[...] = jnp.zeros_like(acc)

    def gate_up(f, squares):
        parts = []
        gain_row = gains[f // 2]
        for m in range(2):
            rows = hid[f, m].reshape(256, 512).astype(F32)
            parts.append(jnp.sum(rows * rows, axis=1, keepdims=True))
            scaled = jnp.concatenate(
                [
                    rows[:, j * 128:(j + 1) * 128]
                    * jnp.where(f % 2 == 0, gain_row[j:j + 1], gain_row[4 + j:5 + j])
                    for j in range(4)
                ],
                axis=1,
            ).astype(BF)
            for s in range(2):
                weights = w_all[f, :, :, s * 384:s * 384 + 256].reshape(512, 256)
                acc[s, m * 256:(m + 1) * 256] += jnp.dot(scaled, weights, preferred_element_type=F32)
        return squares + jnp.concatenate(parts, axis=0)

    squares = lax.fori_loop(0, 8, gate_up, jnp.zeros((512, 1), F32))
    inverse = lax.rsqrt(squares / D + 1e-05)
    for s in range(2):
        gate, up = acc[s, :, :128] * inverse, acc[s, :, 128:] * inverse
        act[:, s * 128:(s + 1) * 128] = (gate / (1.0 + jnp.exp(-gate)) * up).astype(BF)

    def project_down(f, _):
        weights = jnp.concatenate(
            [w_all[f, :, :, s * 384 + 256:s * 384 + 384].reshape(512, 128) for s in range(2)], axis=1
        )
        for m in range(2):
            part = nt(act[m * 256:(m + 1) * 256], weights)
            down[f // 2, f % 2, m] = part.astype(BF).reshape(4, 64, 512)
        return 0

    lax.fori_loop(0, 8, project_down, 0)

    right_sid, left_sid, x_sid, y_sid, odd_sid = new(7), new(7), new(4), new(8), new(4)

    def odd(i, b):
        return down.at[i % 4, 1, i // 4, pl.ds(b * 2, 2)]

    to_right, to_left = to_y((y + 1) % NY), to_y((y + NY - 1) % NY)
    push(odd((y + NY - 1) % NY, 0), ring_r.at[0], right_sid, to_right)
    push(odd((y + 1) % NY, 1), ring_l.at[0], left_sid, to_left)
    for k in range(1, NX):
        peer = (x + k) % NX
        push(down.at[:, 0, :, peer], x_in.at[k - 1], x_sid + k, to_x(peer))

    def add_even():
        for k in range(1, NX):
            arrive(x_in.at[k - 1], x_sid + k)

        def add(i, _):
            total = down[i // 2, 0, i % 2, x].astype(F32)
            for k in range(3):
                total += x_in[k, i // 2, i % 2].astype(F32)
            x_sum[i // 2, i % 2] = total.astype(BF)
            return 0

        lax.fori_loop(0, 8, add, 0)
        for k in range(1, NY):
            peer = (y + k) % NY
            push(x_sum.at[peer % 4, peer // 4], y_in.at[k - 1], y_sid + k, to_y(peer))

    for s in range(7):
        if s == 5:
            add_even()
        back, ahead = (y + 2 * NY - 2 - s) % NY, (y + 2 + s) % NY
        for buf, sid, i, b, dev in (
            (ring_r, right_sid, back, 0, to_right), (ring_l, left_sid, ahead, 1, to_left)
        ):
            arrive(buf.at[s], sid + s)
            mine = down[i % 4, 1, i // 4, pl.ds(b * 2, 2)]
            total = (buf[s].astype(F32) + mine.astype(F32)).astype(BF)
            if s < 6:
                buf[s] = total
                push(buf.at[s], buf.at[s + 1], sid + s + 1, dev)
            else:
                odd_sum[b * 2:b * 2 + 2] = total
    for k in range(1, NX):
        peer = (x + k) % NX
        push(odd_sum.at[peer], odd_in.at[k - 1], odd_sid + k, to_x(peer))

    total = x_sum[y_lo, y_hi].astype(F32)
    for k in range(1, NY):
        arrive(y_in.at[k - 1], y_sid + k)
        total += y_in[k - 1].astype(F32)
    out_ref[:, :512] = (hid[2 * y_lo, y_hi, x].astype(F32) + total).astype(BF)
    total = odd_sum[x].astype(F32)
    for k in range(1, NX):
        arrive(odd_in.at[k - 1], odd_sid + k)
        total += odd_in[k - 1].astype(F32)
    out_ref[:, 512:] = (hid[2 * y_lo + 1, y_hi, x].astype(F32) + total).astype(BF)

    for copy in sends:
        copy.wait_send()
    for k in range(1, NY):
        peer = (y + k) % NY

        @pl.when(peer != NY - 1)
        def _(k=k, peer=peer):
            for part, src in enumerate(w_sources(peer)):
                remote(
                    src, w_all.at[feat(y), z, :, w_cols(part, c)], w_sid + 3 * k + part, to_y(peer)
                ).wait_send()

    assert counter[0] <= SEMS, counter[0]


SEMS = 256


def per_device(query, key, value, doc_lengths, resid, norm_gain, w_out, w_gate_up, w_down):
    vmem = pl.BlockSpec(memory_space=pltpu.VMEM)
    anywhere = pl.BlockSpec(memory_space=pl.ANY)
    smem = pl.BlockSpec(memory_space=pltpu.SMEM)

    def buf(*shape, kind=BF):
        return pltpu.VMEM(shape, kind)

    return pl.pallas_call(
        kernel,
        out_shape=(
            jax.ShapeDtypeStruct((128, 512), BF),
            jax.ShapeDtypeStruct((64, 1024), BF),
        ),
        in_specs=[vmem, vmem, vmem, smem, anywhere, vmem, anywhere, anywhere, anywhere],
        out_specs=(vmem, vmem),
        scratch_shapes=[
            buf(8, 16, 512),
            buf(BACK, 8, 2, 8, 16, 128),
            buf(4, 128, BACK * 512, kind=F32),
            buf(8, 64, 1024),
            buf(8, 64, 1024),
            buf(8, 8, 64, 768),
            buf(2, 64, 512),
            buf(4, 8, 128, kind=F32),
            buf(2, 4, 64, 512),
            buf(3, 2, 64, 512),
            buf(8, 2, 4, 64, 512),
            buf(2, 512, 256, kind=F32),
            buf(512, 256),
            buf(4, 2, 2, 4, 64, 512),
            buf(3, 4, 2, 64, 512),
            buf(4, 2, 64, 512),
            buf(7, 64, 512),
            buf(7, 2, 64, 512),
            buf(7, 2, 64, 512),
            buf(4, 64, 512),
            buf(3, 64, 512),
            pltpu.SemaphoreType.DMA((SEMS,)),
            pltpu.SemaphoreType.DMA((SEMS,)),
            pltpu.SemaphoreType.DMA((16,)),
        ],
        compiler_params=pltpu.CompilerParams(
            collective_id=0, has_side_effects=True, vmem_limit_bytes=56 * 1024 * 1024
        ),
        cost_estimate=pl.CostEstimate(flops=4_000_000_000, bytes_accessed=4_000_000, transcendentals=2_000_000),
    )(
        query, key, value, doc_lengths, resid, norm_gain.reshape(8, 128),
        w_out.T, w_gate_up, w_down.T,
    )


def solution(mesh):
    placed = (
        P(("outer", "inner", "head"), None),
        P(("outer", "inner", "head"), None),
        P(("outer", "inner", "head"), None),
        P(),
        P("outer", "inner"),
        P("inner"),
        P("head", ("inner", "outer")),
        P(None, ("inner", "outer"), "head"),
        P("head", ("inner", "outer")),
    )
    return jax.shard_map(
        per_device,
        mesh=mesh,
        in_specs=placed,
        out_specs=(P(("outer", "inner"), "head"), P(("outer", "head"), "inner")),
        check_vma=False,
    )
```

```python
import jax
import jax.numpy as jnp
from jax import lax
from jax.experimental import pallas as pl
from jax.experimental.pallas import tpu as pltpu
from jax.sharding import PartitionSpec as P

MESH = pl.DeviceIdType.MESH
D = 4096
BF = jnp.bfloat16
F32 = jnp.float32
SCALE = 128 ** (-0.5)
DOCS = 24
NX, NY, NZ = 4, 8, 8
BACK = 5


def nt(a, b):
    return lax.dot_general(a, b, (((1,), (1,)), ((), ())), preferred_element_type=F32)


def kernel(
    q_ref, k_ref, v_ref, docs_ref, resid_ref, gain_ref, wo_ref, wgu_ref, wd_ref,
    ctx_ref, out_ref,
    q_all, keys_all, values_near, values_far, relay, scores, ctx_all, wo_all, w_all, res, gains,
    proj, proj_in, hid, acc, act, down, x_in, x_sum, y_in, rings, odd_sum, odd_in,
    send_sem, recv_sem, local_sem,
):
    head = lax.axis_index("head")
    y_lo = lax.axis_index("inner")
    outer = lax.axis_index("outer")
    x, c = head // 2, head % 2
    u, pair, mirror = x % 2, x + 1 - 2 * (x % 2), 3 - x
    y_hi, z = outer // NZ, outer % NZ
    y = y_hi * 4 + y_lo
    other = 1 - c

    def to_head(h):
        return {"head": h}

    def to_x(i):
        return {"head": i * 2 + c}

    def to_y(i):
        return {"inner": i % 4, "outer": (i // 4) * NZ + z}

    def to_z(i):
        return {"outer": y_hi * NZ + i}

    def to_outer(i):
        return {"outer": i}

    def to_lo(i):
        return {"inner": i}

    sibling = to_head(x * 2 + other)

    def feat(i):
        return (i % 4) * 2 + i // 4

    counter = [0]
    sends, locals_ = [], []

    def new(count=1):
        counter[0] += count
        return counter[0] - count

    def remote(src, dst, sid, dev):
        return pltpu.make_async_remote_copy(
            src_ref=src, dst_ref=dst, send_sem=send_sem.at[sid], recv_sem=recv_sem.at[sid],
            device_id=dev, device_id_type=MESH,
        )

    def push(src, dst, sid, dev):
        copy = remote(src, dst, sid, dev)
        copy.start()
        sends.append(copy)

    def arrive(dst, sid):
        remote(dst, dst, sid, sibling).wait_recv()

    local_count = [0]

    def local(src, dst):
        copy = pltpu.make_async_copy(src, dst, local_sem.at[local_count[0]])
        local_count[0] += 1
        copy.start()
        return copy

    def ring(n, me, to, chunk, half, arrived=None):
        steps = n // 2
        sr, sl = new(steps), new(steps)
        right, left = to((me + 1) % n), to((me + n - 1) % n)

        def run():
            for s in range(steps):
                back, ahead = (me - s + n) % n, (me + s) % n
                if s > 0:
                    arrive(chunk(back), sr + s - 1)
                    arrive(chunk(ahead), sl + s - 1)
                if s < steps - 1:
                    push(chunk(back), chunk(back), sr + s, right)
                    push(chunk(ahead), chunk(ahead), sl + s, left)
                else:
                    push(half(back, 0), half(back, 0), sr + s, right)
                    push(half(ahead, 1), half(ahead, 1), sl + s, left)
                if arrived is not None:
                    arrived(back, 2 * s)
                    if s > 0:
                        arrived(ahead, 2 * s - 1)
                yield
            far = (me + steps) % n
            arrive(half(far, 0), sr + steps - 1)
            arrive(half(far, 1), sl + steps - 1)
            if arrived is not None:
                arrived(far, 2 * steps - 1)

        return run()

    def finish(gen):
        for _ in gen:
            pass

    def together(gens):
        for _ in range(5):
            for gen in gens:
                next(gen, None)

    def lanes(core, width):
        return pl.ds(pl.multiple_of(core * width, width), width)

    barrier = pltpu.get_barrier_semaphore()
    for k in range(1, 8):
        pl.semaphore_signal(barrier, inc=1, device_id=to_head((head + k) % 8), device_id_type=MESH)
        pl.semaphore_signal(barrier, inc=1, device_id=to_y((y + k) % NY), device_id_type=MESH)
    for k in range(1, BACK):
        for peer in ((outer + k) % 16, (outer + 16 - k) % 16):
            pl.semaphore_signal(barrier, inc=1, device_id=to_outer(peer), device_id_type=MESH)
        pl.semaphore_signal(barrier, inc=1, device_id=to_z((z + k) % NZ), device_id_type=MESH)
        pl.semaphore_signal(barrier, inc=1, device_id=to_z((z + NZ - k) % NZ), device_id_type=MESH)
    pl.semaphore_wait(barrier, 30)

    kv_sid, q_sid = new(16), new(8)
    for k in range(1, 8):
        peer = (head + k) % 8
        cols = pl.ds(pl.multiple_of(peer * 128, 128), 128)
        push(k_ref.at[:, cols], keys_all.at[0, y_lo, head], kv_sid + k, to_head(peer))
        push(v_ref.at[:, cols], values_near.at[y, head], kv_sid + 8 + k, to_head(peer))
    own = pl.ds(pl.multiple_of(head * 128, 128), 128)
    keys_all[0, y_lo, head] = k_ref[:, own]
    values_near[y, head] = v_ref[:, own]
    for k in range(1, 8):
        peer = (head + k) % 8
        cols = pl.ds(pl.multiple_of(peer * 512, 512), 512)
        push(q_ref.at[:, cols], q_all.at[head], q_sid + k, to_head(peer))
    q_all[head] = q_ref[:, pl.ds(pl.multiple_of(head * 512, 512), 512)]

    w_sid = new(24)

    def w_cols(part, s):
        return pl.ds(pl.multiple_of(s * 768 + part * 128, 128), 128)

    def w_sources(i):
        cols = pl.ds(pl.multiple_of(i * 128, 128), 128)
        return wgu_ref.at[0, :, cols], wgu_ref.at[1, :, cols], wd_ref.at[:, cols]

    def w_exchange(parts):
        for k in range(1, NY):
            peer = (y + k) % NY

            @pl.when(peer != NY - 1)
            def _(k=k, peer=peer):
                for part in parts:
                    remote(
                        w_sources(peer)[part], w_all.at[feat(y), z, :, w_cols(part, c)],
                        w_sid + 3 * k + part, to_y(peer),
                    ).start()

    def w_own(part):
        return pltpu.make_async_copy(
            w_sources(y)[part], w_all.at[feat(y), z, :, w_cols(part, c)], local_sem.at[8 + part]
        )

    def w_exchanged(parts):
        @pl.when(y != NY - 1)
        def _():
            for part in parts:
                w_own(part).wait()
                for k in range(1, NY):
                    dst = w_all.at[feat((y + NY - k) % NY), z, :, w_cols(part, c)]
                    arrive(dst, w_sid + 3 * k + part)

    @pl.when(y != NY - 1)
    def _():
        for part in range(3):
            w_own(part).start()

    @pl.when(y == NY - 1)
    def _():
        def zero(f, _):
            w_all[f, z, :, pl.ds(pl.multiple_of(c * 768, 128), 384)] = jnp.zeros((64, 384), BF)
            return 0

        lax.fori_loop(0, 8, zero, 0)

    w_exchange([2])

    for k in range(1, 8):
        peer = (head + 8 - k) % 8
        arrive(keys_all.at[0, y_lo, peer], kv_sid + k)
        arrive(values_near.at[y, peer], kv_sid + 8 + k)

    def shared_ring(buf_chunk, buf_half, then=None):
        sid = new(8)

        def arrived(i, n):
            push(buf_chunk(i, c), buf_chunk(i, c), sid + n, sibling)
            if then is not None:
                then(i, n)

        gen = ring(
            NZ, z, to_z, lambda i: buf_chunk(i, c), lambda i, b: buf_half(i, b, c), arrived
        )

        def wait_sibling():
            for n in range(8):
                step = (n + 1) // 2
                i = (z + step) % NZ if n % 2 else (z - step + NZ) % NZ
                arrive(buf_chunk(i, other), sid + n)

        return gen, wait_sibling

    wo_copy = local(wo_ref, wo_all.at[z, :, lanes(c, 512)])
    wo_ring, wo_wait = shared_ring(
        lambda i, s: wo_all.at[i, :, lanes(s, 512)],
        lambda i, b, s: wo_all.at[i, pl.ds(b * 32, 32), lanes(s, 512)],
    )

    ahead_sid, key_sid, near_sid, far_sid = new(BACK), new(4 * BACK), new(8), new(BACK + 1)

    def key_lo(dz):
        for k in range(1, 4):
            push(keys_all.at[dz, y_lo], keys_all.at[dz, y_lo], key_sid + 4 * dz + k, to_lo((y_lo + k) % 4))

    for k in range(1, NY):
        push(values_near.at[y], values_near.at[y], near_sid + k, to_y((y + k) % NY))
    for dz in range(1, BACK):
        push(keys_all.at[0, y_lo], keys_all.at[dz, y_lo], ahead_sid + dz, to_outer((outer + dz) % 16))
    key_lo(0)
    wo_copy.wait()
    next(wo_ring)
    for k in range(1, NY):
        arrive(values_near.at[(y + NY - k) % NY], near_sid + k)

    def row_blocks(dz):
        return values_near.at[pl.ds(jnp.where(z + dz < NZ, y_hi, 1 - y_hi) * 4, 4)]

    push(row_blocks(4), relay, far_sid, to_z((z + NZ - 2) % NZ))
    for dz in range(1, 4):
        push(row_blocks(dz), values_far.at[dz - 1], far_sid + dz, to_z((z + dz) % NZ))
    for dz in range(1, 3):
        arrive(keys_all.at[dz, y_lo], ahead_sid + dz)
        key_lo(dz)
    next(wo_ring)
    arrive(relay, far_sid)
    push(relay, values_far.at[3], far_sid + 4, to_z((z + NZ - 2) % NZ))
    for dz in range(3, BACK):
        arrive(keys_all.at[dz, y_lo], ahead_sid + dz)
        key_lo(dz)
    w_exchange([0, 1])

    res_rows = pl.ds(pl.multiple_of(head * 64, 64), 64)
    res_sid = new()
    push(
        resid_ref.at[res_rows, lanes(1 - y_hi, 512)], res.at[y_hi], res_sid,
        to_y((1 - y_hi) * 4 + y_lo),
    )
    res_copy = local(resid_ref.at[res_rows, lanes(y_hi, 512)], res.at[y_hi])
    gain_sid = new(4)
    for k in range(1, 4):
        push(gain_ref, gains.at[y_lo], gain_sid + k, to_y(y_hi * 4 + (y_lo + k) % 4))
    gains[y_lo] = gain_ref[...]

    def w_part(i, s, first, width):
        return w_all.at[:, i, :, pl.ds(pl.multiple_of(s * 768 + first, 128), width)]

    over_sid, mirror_sid, w_core_sid = new(), new(8), new(8)
    to_mirror = to_x(mirror)
    w_exchanged([2])
    push(w_part(z, c, 256, 128), w_part(z, c, 384, 128), over_sid, to_mirror)
    next(wo_ring)
    next(wo_ring)
    for dz in range(1, BACK):
        arrive(values_far.at[dz - 1], far_sid + dz)
    for dz in range(BACK):
        for k in range(1, 4):
            arrive(keys_all.at[dz, (y_lo + 4 - k) % 4], key_sid + 4 * dz + k)

    for k in range(1, 8):
        arrive(q_all.at[(head + 8 - k) % 8], q_sid + k)
    place = outer * 512 + y_lo * 128 + lax.broadcasted_iota(jnp.int32, (128, 1), 0)
    start = jnp.zeros((128, 1), jnp.int32)
    bound = jnp.int32(0)
    for j in range(DOCS):
        bound = bound + docs_ref[j]
        start = jnp.where(bound <= place, bound, start)
    for dz in range(BACK):
        keys = keys_all[dz].reshape(512, 128)
        key_place = (outer - dz) * 512 + lax.broadcasted_iota(jnp.int32, (1, 512), 1)
        bias = jnp.where((key_place <= place) & (key_place >= start), 0.0, -1e30)
        for g in range(4):
            heads_q = q_all[:, :, g * 128:(g + 1) * 128].reshape(128, 128)
            scores[g, :, dz * 512:(dz + 1) * 512] = nt(heads_q, keys) * SCALE + bias
    for g in range(4):
        s = scores[g]
        e = jnp.exp(s - jnp.max(s, axis=1, keepdims=True))
        total = jnp.sum(e, axis=1, keepdims=True)
        e = e.astype(BF)
        summed = jnp.zeros((128, 128), F32)
        for dz in range(BACK):
            values = (values_near[pl.ds(y_hi * 4, 4)] if dz == 0 else values_far[dz - 1]).reshape(512, 128)
            summed += jnp.dot(e[:, dz * 512:(dz + 1) * 512], values, preferred_element_type=F32)
        ctx_ref[:, g * 128:(g + 1) * 128] = (summed / total).astype(BF)

    def half_rows(i):
        return pl.ds(pl.multiple_of(i * 64, 64), 64)

    ctx_sid = new()
    push(ctx_ref.at[half_rows(other)], ctx_all.at[y, :, lanes(c, 512)], ctx_sid, sibling)
    ctx_all[y, :, lanes(c, 512)] = ctx_ref[half_rows(c), :]

    w_exchanged([0, 1])
    arrive(w_part(z, c, 384, 128), over_sid)

    def w_arrived(i, n):
        push(w_part(i, c, 0, 256), w_part(i, c, 512, 256), mirror_sid + n, to_mirror)

    w_ring, w_wait = shared_ring(
        lambda i, s: w_part(i, s, 0, 512),
        lambda i, b, s: w_all.at[pl.ds(b * 4, 4), i, :, pl.ds(pl.multiple_of(s * 768, 128), 512)],
        w_arrived,
    )
    next(w_ring)

    def w_place(n):
        step = (n + 1) // 2
        return (z + step) % NZ if n % 2 else (z - step + NZ) % NZ

    def w_mirrored(*which):
        for n in which:
            gate_up_part = w_part(w_place(n), c, 512, 256)
            arrive(gate_up_part, mirror_sid + n)
            push(gate_up_part, gate_up_part, w_core_sid + n, sibling)

    arrive(ctx_all.at[y, :, lanes(other, 512)], ctx_sid)
    proj_sid = new(8)

    def proj_push(i):
        way = (i % 4 + NX - x) % NX
        return remote(
            proj.at[i], proj_in.at[way, i // 4], proj_sid + way * 2 + i // 4, to_x(i % 4)
        )

    def project(i, n):
        proj[i] = nt(ctx_all[i], wo_all[...].reshape(512, 1024)).astype(BF)

        @pl.when(i % 4 != x)
        def _():
            proj_push(i).start()

    finish(wo_ring)
    wo_wait()
    together([
        ring(
            NY, y, to_y, lambda i, p=p: ctx_all.at[i, pl.ds(p * 32, 32)],
            lambda i, b, p=p: ctx_all.at[i, pl.ds(p * 32 + b * 16, 16)],
            project if p else None,
        )
        for p in range(2)
    ])
    next(w_ring)
    w_mirrored(0)
    res_copy.wait()
    arrive(res.at[1 - y_hi], res_sid)
    for k in range(1, NX):
        for g in range(2):
            arrive(proj_in.at[k, g], proj_sid + 2 * k + g)
    for g in range(2):
        total = proj[g * 4 + x].astype(F32)
        for k in range(1, NX):
            total += proj_in[k, g].astype(F32)
        hid[feat(y), g, u] = (res[g].astype(F32) + total).astype(BF)

    first_sid, second_sid = new(), new(8)
    to_pair = to_x(pair)

    def along_x(i, n):
        push(hid.at[feat(i), 1, u], hid.at[feat(i), 1, u], second_sid + n, to_pair)

    push(hid.at[feat(y), 0, u], hid.at[feat(y), 0, u], first_sid, to_pair)
    y_first = ring(
        NY, y, to_y, lambda i: hid.at[feat(i), 1, u],
        lambda i, b: hid.at[feat(i), 1, u, pl.ds(b * 32, 32)], along_x,
    )
    next(y_first)
    arrive(hid.at[feat(y), 0, 1 - u], first_sid)
    x_first = [
        ring(
            NY, y, to_y, lambda i, p=p: hid.at[feat(i), 0, p],
            lambda i, b, p=p: hid.at[feat(i), 0, p, pl.ds(b * 32, 32)],
        )
        for p in range(2)
    ]
    for s in range(4):
        next(x_first[0])
        next(x_first[1])
        next(y_first, None)
        if s in (0, 2):
            next(w_ring)
            w_mirrored(*((1, 2) if s == 0 else (3, 4)))
    for gen in x_first:
        next(gen, None)
    for n in range(8):
        step = (n + 1) // 2
        i = (y + step) % NY if n % 2 else (y - step + NY) % NY
        arrive(hid.at[feat(i), 1, 1 - u], second_sid + n)
    finish(w_ring)
    w_mirrored(5, 6, 7)
    for n in range(8):
        arrive(w_part(w_place(n), other, 512, 256), w_core_sid + n)
    for k in range(1, 4):
        arrive(gains.at[(y_lo + 4 - k) % 4], gain_sid + k)
    w_wait()

    acc[...] = jnp.zeros_like(acc)

    def gate_up(f, squares):
        gain_row = gains[f // 2]
        rows = hid[f].reshape(256, 512).astype(F32)
        scaled = jnp.concatenate(
            [
                rows[:, j * 128:(j + 1) * 128]
                * jnp.where(f % 2 == 0, gain_row[j:j + 1], gain_row[4 + j:5 + j])
                for j in range(4)
            ],
            axis=1,
        ).astype(BF)
        for s, first in enumerate(SLOTS):
            weights = w_all[f, :, :, first:first + 256].reshape(512, 256)
            acc[s] += jnp.dot(scaled, weights, preferred_element_type=F32)
        return squares + jnp.sum(rows * rows, axis=1, keepdims=True)

    squares = lax.fori_loop(0, 8, gate_up, jnp.zeros((256, 1), F32))
    inverse = lax.rsqrt(squares / D + 1e-05)
    for s in range(4):
        gate, up = acc[s, :, :128] * inverse, acc[s, :, 128:] * inverse
        act[:, s * 128:(s + 1) * 128] = (gate / (1.0 + jnp.exp(-gate)) * up).astype(BF)

    def project_down(f, _):
        weights = jnp.concatenate(
            [w_all[f, :, :, s * 768 + 256:s * 768 + 512].reshape(512, 256) for s in range(2)], axis=1
        )
        down[f // 2, f % 2] = nt(act[...], weights).astype(BF).reshape(2, 2, 64, 512)
        return 0

    lax.fori_loop(0, 8, project_down, 0)

    ring_sid, x_sid, y_sid, odd_sid = new(16), new(4), new(8), new()
    for k in range(4):
        piece = down.at[(y_lo + k) % 4, 0, :, 1 - u]
        push(piece, x_in.at[k], x_sid + k, to_pair)

    def odd(i, p, first, count):
        return down.at[i % 4, 1, i // 4, p, pl.ds(first, count)]

    def add_even(k):
        arrive(x_in.at[k], x_sid + k)
        for g in range(2):
            mine = down[(y_lo + k) % 4, 0, g, u]
            x_sum[k, g] = (mine.astype(F32) + x_in[k, g].astype(F32)).astype(BF)
        for way in (k, k + 4):
            if way > 0:
                peer = (y + way) % NY
                push(x_sum.at[k, peer // 4], y_in.at[way - 1], y_sid + way, to_y(peer))

    to_right, to_left = to_y((y + 1) % NY), to_y((y + NY - 1) % NY)
    for s in range(4):
        for p in range(2):
            for way in range(2):
                slots, sid = rings.at[way, p], ring_sid + 8 * way + 4 * p
                i = (y + 4 - s) % NY if way == 0 else (y + 4 + s) % NY
                dev = to_right if way == 0 else to_left
                half = pl.ds(32 * way, 32)
                if s == 0:
                    push(odd(i, p, 32 * way, 32), slots.at[0, half], sid, dev)
                    continue
                if s == 1:
                    rest = pl.ds(32 * (1 - way), 32)
                    arrive(slots.at[0, half], sid)
                    slots[0, half] = (slots[0, half].astype(F32) + odd(i, p, 32 * way, 32)[...].astype(F32)).astype(BF)
                    slots[0, rest] = odd(i, p, 32 * (1 - way), 32)[...]
                else:
                    arrive(slots.at[s - 1], sid + s - 1)
                    slots[s - 1] = (slots[s - 1].astype(F32) + odd(i, p, 0, 64)[...].astype(F32)).astype(BF)
                push(slots.at[s - 1], slots.at[s], sid + s, dev)
        add_even(s)
    for p in range(2):
        total = odd(y, p, 0, 64)[...].astype(F32)
        for way in range(2):
            sid = ring_sid + 8 * way + 4 * p + 3
            arrive(rings.at[way, p, 3], sid)
            total += rings[way, p, 3].astype(F32)
        odd_sum[p] = total.astype(BF)
    push(odd_sum.at[1 - u], odd_in, odd_sid, to_pair)

    total = x_sum[0, y_hi].astype(F32)
    for k in range(1, NY):
        arrive(y_in.at[k - 1], y_sid + k)
        total += y_in[k - 1].astype(F32)
    out_ref[:, :512] = (hid[2 * y_lo, y_hi, u].astype(F32) + total).astype(BF)
    arrive(odd_in, odd_sid)
    total = odd_sum[u].astype(F32) + odd_in[...].astype(F32)
    out_ref[:, 512:] = (hid[2 * y_lo + 1, y_hi, u].astype(F32) + total).astype(BF)

    for copy in sends:
        copy.wait_send()
    for i in range(NY):
        @pl.when(i % 4 != x)
        def _(i=i):
            proj_push(i).wait_send()

    for k in range(1, NY):
        peer = (y + k) % NY

        @pl.when(peer != NY - 1)
        def _(k=k, peer=peer):
            for part, src in enumerate(w_sources(peer)):
                remote(
                    src, w_all.at[feat(y), z, :, w_cols(part, c)], w_sid + 3 * k + part, to_y(peer)
                ).wait_send()

    assert counter[0] <= SEMS, counter[0]


SEMS = 320
SLOTS = (0, 512, 768, 1280)


def per_device(query, key, value, doc_lengths, resid, norm_gain, w_out, w_gate_up, w_down):
    vmem = pl.BlockSpec(memory_space=pltpu.VMEM)
    anywhere = pl.BlockSpec(memory_space=pl.ANY)
    smem = pl.BlockSpec(memory_space=pltpu.SMEM)

    def buf(*shape, kind=BF):
        return pltpu.VMEM(shape, kind)

    return pl.pallas_call(
        kernel,
        out_shape=(
            jax.ShapeDtypeStruct((128, 512), BF),
            jax.ShapeDtypeStruct((64, 1024), BF),
        ),
        in_specs=[vmem, vmem, vmem, smem, anywhere, vmem, anywhere, anywhere, anywhere],
        out_specs=(vmem, vmem),
        scratch_shapes=[
            buf(8, 16, 512),
            buf(BACK, 4, 8, 16, 128),
            buf(8, 8, 16, 128),
            buf(BACK - 1, 4, 8, 16, 128),
            buf(4, 8, 16, 128),
            buf(4, 128, BACK * 512, kind=F32),
            buf(8, 64, 1024),
            buf(8, 64, 1024),
            buf(8, 8, 64, 1536),
            buf(2, 64, 512),
            buf(4, 8, 128, kind=F32),
            buf(8, 64, 512),
            buf(4, 2, 64, 512),
            buf(8, 2, 2, 64, 512),
            buf(4, 256, 256, kind=F32),
            buf(256, 512),
            buf(4, 2, 2, 2, 64, 512),
            buf(4, 2, 64, 512),
            buf(4, 2, 64, 512),
            buf(7, 64, 512),
            buf(2, 2, 4, 64, 512),
            buf(2, 64, 512),
            buf(64, 512),
            pltpu.SemaphoreType.DMA((SEMS,)),
            pltpu.SemaphoreType.DMA((SEMS,)),
            pltpu.SemaphoreType.DMA((16,)),
        ],
        compiler_params=pltpu.CompilerParams(
            collective_id=0, has_side_effects=True, vmem_limit_bytes=56 * 1024 * 1024
        ),
        cost_estimate=pl.CostEstimate(flops=4_000_000_000, bytes_accessed=4_000_000, transcendentals=2_000_000),
    )(
        query, key, value, doc_lengths, resid, norm_gain.reshape(8, 128),
        w_out.T, w_gate_up, w_down.T,
    )


def solution(mesh):
    placed = (
        P(("outer", "inner", "head"), None),
        P(("outer", "inner", "head"), None),
        P(("outer", "inner", "head"), None),
        P(),
        P("outer", "inner"),
        P("inner"),
        P("head", ("inner", "outer")),
        P(None, ("inner", "outer"), "head"),
        P("head", ("inner", "outer")),
    )
    return jax.shard_map(
        per_device,
        mesh=mesh,
        in_specs=placed,
        out_specs=(P(("outer", "inner"), "head"), P(("outer", "head"), "inner")),
        check_vma=False,
    )
```

```python
import jax
import jax.numpy as jnp
from jax import lax
from jax.experimental import pallas as pl
from jax.experimental.pallas import tpu as pltpu
from jax.sharding import PartitionSpec as P

MESH = pl.DeviceIdType.MESH
D = 4096
BF = jnp.bfloat16
F32 = jnp.float32
SCALE = 128 ** (-0.5)
DOCS = 24
NX, NY, NZ = 4, 8, 8
BACK = 5


def nt(a, b):
    return lax.dot_general(a, b, (((1,), (1,)), ((), ())), preferred_element_type=F32)


def kernel(
    q_ref, k_ref, v_ref, docs_ref, resid_ref, gain_ref, wo_ref, wgu_ref, wd_ref,
    ctx_ref, out_ref,
    q_all, keys_all, values_near, values_far, relay, scores, ctx_all, wo_all, w_all, res, gains,
    proj, proj_in, hid, acc, act, down, x_in, x_sum, rings, odd_sum, odd_in,
    send_sem, recv_sem, local_sem,
):
    head = lax.axis_index("head")
    y_lo = lax.axis_index("inner")
    outer = lax.axis_index("outer")
    x, c = head // 2, head % 2
    u, pair, mirror = x % 2, x + 1 - 2 * (x % 2), 3 - x
    y_hi, z = outer // NZ, outer % NZ
    y = y_hi * 4 + y_lo
    other = 1 - c

    def to_head(h):
        return {"head": h}

    def to_x(i):
        return {"head": i * 2 + c}

    def to_y(i):
        return {"inner": i % 4, "outer": (i // 4) * NZ + z}

    def to_z(i):
        return {"outer": y_hi * NZ + i}

    def to_outer(i):
        return {"outer": i}

    def to_lo(i):
        return {"inner": i}

    def to_cross(i):
        return {"head": x * 2 + other, "inner": i}

    sibling = to_head(x * 2 + other)

    def feat(i):
        return (i % 4) * 2 + i // 4

    counter = [0]
    sends, locals_ = [], []

    def new(count=1):
        counter[0] += count
        return counter[0] - count

    def remote(src, dst, sid, dev):
        return pltpu.make_async_remote_copy(
            src_ref=src, dst_ref=dst, send_sem=send_sem.at[sid], recv_sem=recv_sem.at[sid],
            device_id=dev, device_id_type=MESH,
        )

    def push(src, dst, sid, dev):
        copy = remote(src, dst, sid, dev)
        copy.start()
        sends.append(copy)

    maybes = []

    def push_if(cond, *args):
        @pl.when(cond)
        def _():
            remote(*args).start()

        maybes.append((cond, args))

    def arrive_if(cond, *args):
        @pl.when(cond)
        def _():
            arrive(*args)

    def arrive(dst, sid):
        remote(dst, dst, sid, sibling).wait_recv()

    local_count = [0]

    def local(src, dst):
        copy = pltpu.make_async_copy(src, dst, local_sem.at[local_count[0]])
        local_count[0] += 1
        copy.start()
        return copy

    def ring(n, me, to, chunk, half, arrived=None):
        steps = n // 2
        sr, sl = new(steps), new(steps)
        right, left = to((me + 1) % n), to((me + n - 1) % n)

        def run():
            for s in range(steps):
                back, ahead = (me - s + n) % n, (me + s) % n
                if s > 0:
                    arrive(chunk(back), sr + s - 1)
                    arrive(chunk(ahead), sl + s - 1)
                if s < steps - 1:
                    push(chunk(back), chunk(back), sr + s, right)
                    push(chunk(ahead), chunk(ahead), sl + s, left)
                elif half is None:
                    push(chunk(ahead), chunk(ahead), sl + s, left)
                else:
                    push(half(back, 0), half(back, 0), sr + s, right)
                    push(half(ahead, 1), half(ahead, 1), sl + s, left)
                if arrived is not None:
                    arrived(back, 2 * s)
                    if s > 0:
                        arrived(ahead, 2 * s - 1)
                yield
            far = (me + steps) % n
            if half is None:
                arrive(chunk(far), sl + steps - 1)
            else:
                arrive(half(far, 0), sr + steps - 1)
                arrive(half(far, 1), sl + steps - 1)
            if arrived is not None:
                arrived(far, 2 * steps - 1)

        return run()

    def finish(gen):
        for _ in gen:
            pass

    def together(gens):
        for _ in range(5):
            for gen in gens:
                next(gen, None)

    def lanes(core, width):
        return pl.ds(pl.multiple_of(core * width, width), width)

    keys_all[...] = jnp.zeros_like(keys_all)
    values_near[...] = jnp.zeros_like(values_near)

    barrier = pltpu.get_barrier_semaphore()
    for k in range(1, 8):
        pl.semaphore_signal(barrier, inc=1, device_id=to_head((head + k) % 8), device_id_type=MESH)
        pl.semaphore_signal(barrier, inc=1, device_id=to_y((y + k) % NY), device_id_type=MESH)
    for k in range(1, BACK):
        for peer in ((outer + k) % 16, (outer + 16 - k) % 16):
            pl.semaphore_signal(barrier, inc=1, device_id=to_outer(peer), device_id_type=MESH)
        pl.semaphore_signal(barrier, inc=1, device_id=to_z((z + k) % NZ), device_id_type=MESH)
        pl.semaphore_signal(barrier, inc=1, device_id=to_z((z + NZ - k) % NZ), device_id_type=MESH)
    for k in range(1, 4):
        pl.semaphore_signal(barrier, inc=1, device_id=to_cross((y_lo + k) % 4), device_id_type=MESH)
    pl.semaphore_wait(barrier, 33)

    kv_sid, q_sid = new(16), new(8)
    for k in range(1, 8):
        peer = (head + k) % 8
        cols = pl.ds(pl.multiple_of(peer * 128, 128), 128)
        push(k_ref.at[:, cols], keys_all.at[0, y_lo, head], kv_sid + k, to_head(peer))
        push(v_ref.at[:, cols], values_near.at[y, head], kv_sid + 8 + k, to_head(peer))
    own = pl.ds(pl.multiple_of(head * 128, 128), 128)
    own_copies = [
        local(k_ref.at[:, own], keys_all.at[0, y_lo, head]),
        local(v_ref.at[:, own], values_near.at[y, head]),
    ]
    for k in range(1, 8):
        peer = (head + k) % 8
        cols = pl.ds(pl.multiple_of(peer * 512, 512), 512)
        push(q_ref.at[:, cols], q_all.at[head], q_sid + k, to_head(peer))
    own_copies.append(local(q_ref.at[:, pl.ds(pl.multiple_of(head * 512, 512), 512)], q_all.at[head]))

    w_sid = new(24)

    def w_cols(part, s):
        return pl.ds(pl.multiple_of(s * 768 + part * 128, 128), 128)

    def w_sources(i):
        cols = pl.ds(pl.multiple_of(i * 128, 128), 128)
        return wgu_ref.at[0, :, cols], wgu_ref.at[1, :, cols], wd_ref.at[:, cols]

    def w_exchange(parts):
        for k in range(1, NY):
            peer = (y + k) % NY

            @pl.when(peer != NY - 1)
            def _(k=k, peer=peer):
                for part in parts:
                    remote(
                        w_sources(peer)[part], w_all.at[feat(y), z, :, w_cols(part, c)],
                        w_sid + 3 * k + part, to_y(peer),
                    ).start()

    def w_own(part):
        return pltpu.make_async_copy(
            w_sources(y)[part], w_all.at[feat(y), z, :, w_cols(part, c)], local_sem.at[8 + part]
        )

    def w_exchanged(parts):
        @pl.when(y != NY - 1)
        def _():
            for part in parts:
                w_own(part).wait()
                for k in range(1, NY):
                    dst = w_all.at[feat((y + NY - k) % NY), z, :, w_cols(part, c)]
                    arrive(dst, w_sid + 3 * k + part)

    @pl.when(y != NY - 1)
    def _():
        for part in range(3):
            w_own(part).start()

    @pl.when(y == NY - 1)
    def _():
        def zero(f, _):
            w_all[f, z, :, pl.ds(pl.multiple_of(c * 768, 128), 384)] = jnp.zeros((64, 384), BF)
            return 0

        lax.fori_loop(0, 8, zero, 0)

    wo_sid = new()
    push(wo_ref, wo_all.at[y_hi, z, :, lanes(c, 512)], wo_sid, to_y((1 - y_hi) * 4 + y_lo))
    wo_copy = local(wo_ref, wo_all.at[y_hi, z, :, lanes(c, 512)])
    res_copy = local(resid_ref.at[pl.ds(pl.multiple_of(head * 64, 64), 64)], res)

    for copy in own_copies:
        copy.wait()
    for k in range(1, 8):
        peer = (head + 8 - k) % 8
        arrive(keys_all.at[0, y_lo, peer], kv_sid + k)
        arrive(values_near.at[y, peer], kv_sid + 8 + k)

    def shared_ring(buf_chunk, then=None, buf_half=None):
        sid = new(8)

        def arrived(i, n):
            push(buf_chunk(i, c), buf_chunk(i, c), sid + n, sibling)
            if then is not None:
                then(i, n)

        half = None if buf_half is None else lambda i, b: buf_half(i, b, c)
        gen = ring(NZ, z, to_z, lambda i: buf_chunk(i, c), half, arrived)

        def wait_sibling():
            for n in range(8):
                step = (n + 1) // 2
                i = (z + step) % NZ if n % 2 else (z - step + NZ) % NZ
                arrive(buf_chunk(i, other), sid + n)

        return gen, wait_sibling

    wo_ring, wo_wait = shared_ring(
        lambda i, s: wo_all.at[:, i, :, lanes(s, 512)]
    )

    ahead_sid, key_sid, near_sid, far_sid = new(BACK), new(4 * BACK), new(8), new(BACK + 1)

    def key_wanted(dz, src, dst):
        seen = outer >= dz
        return seen & (src < dst) if dz == 0 else seen & (src > dst) if dz == 4 else seen

    def key_lo(dz):
        for k in range(1, 4):
            peer = (y_lo + k) % 4
            push_if(
                key_wanted(dz, y_lo, peer),
                keys_all.at[dz, y_lo], keys_all.at[dz, y_lo], key_sid + 4 * dz + k, to_lo(peer),
            )

    def key_ahead(dz):
        arrive_if(outer >= dz, keys_all.at[dz, y_lo], ahead_sid + dz)

    def near_wanted(row):
        return (row == y_hi) | ((z >= 4) & (row == 0))

    for k in range(1, NY):
        peer = (y + k) % NY
        push_if(
            (peer // 4 == y_hi) | ((z >= 4) & (y_hi == 0)),
            values_near.at[y], values_near.at[y], near_sid + k, to_y(peer),
        )
    for dz in range(1, BACK):
        push_if(
            outer + dz < 16,
            keys_all.at[0, y_lo], keys_all.at[dz, y_lo], ahead_sid + dz, to_outer((outer + dz) % 16),
        )
    key_lo(0)
    wo_copy.wait()
    arrive(wo_all.at[1 - y_hi, z, :, lanes(c, 512)], wo_sid)
    next(wo_ring)
    for k in range(1, NY):
        peer = (y + NY - k) % NY
        arrive_if(near_wanted(peer // 4), values_near.at[peer], near_sid + k)
        if k == 4:
            next(wo_ring)

    def row_blocks(dz):
        return values_near.at[pl.ds(jnp.where(z + dz < NZ, y_hi, 1 - y_hi) * 4, 4)]

    push(row_blocks(4), relay, far_sid, to_z((z + NZ - 2) % NZ))
    for dz in range(1, 3):
        push(row_blocks(dz), values_far.at[dz - 1], far_sid + dz, to_z((z + dz) % NZ))
    push_if(z == NZ - 3, row_blocks(3), values_far.at[2], far_sid + 3, to_z((z + 3) % NZ))
    w_exchange([0, 1, 2])
    for dz in range(1, 3):
        key_ahead(dz)
        key_lo(dz)
    next(wo_ring)
    arrive(values_far.at[1], far_sid + 2)
    push_if(z != NZ - 1, values_far.at[1], values_far.at[2], far_sid + 3, to_z((z + 1) % NZ))
    arrive(relay, far_sid)
    push(relay, values_far.at[3], far_sid + 4, to_z((z + NZ - 2) % NZ))
    for dz in range(3, BACK):
        key_ahead(dz)
        key_lo(dz)

    def w_part(i, s, first, width, f=0, count=8):
        return w_all.at[pl.ds(f, count), i, :, pl.ds(pl.multiple_of(s * 768 + first, 128), width)]

    over_sid, mirror_sid, w_core_sid = new(2), new(24), new(24)
    to_mirror = to_x(mirror)
    next(wo_ring)
    gain_sid = new(4)
    for k in range(1, 4):
        push(gain_ref, gains.at[y_lo], gain_sid + k, to_lo((y_lo + k) % 4))
    gains[y_lo] = gain_ref[...]
    w_exchanged([0, 1, 2])
    push(w_part(z, c, 256, 128), w_part(z, c, 384, 128), over_sid, to_mirror)
    push(w_part(z, c, 0, 256, 6, 2), w_part(z, c, 512, 256, 6, 2), over_sid + 1, to_mirror)

    def w_quarter_ring(p):
        if p == 3:
            return shared_ring(
                lambda i, s: w_part(i, s, 0, 768, 6, 2), None,
                lambda i, b, s: w_part(i, s, 0, 768, 6 + b, 1),
            )

        def w_arrived(i, n):
            push(
                w_part(i, c, 0, 256, 2 * p, 2), w_part(i, c, 512, 256, 2 * p, 2),
                mirror_sid + 8 * p + n, to_mirror,
            )

        return shared_ring(
            lambda i, s: w_part(i, s, 0, 512, 2 * p, 2), w_arrived,
            lambda i, b, s: w_part(i, s, 0, 512, 2 * p + b, 1),
        )

    w_rings = [w_quarter_ring(p) for p in range(4)]

    def w_place(n):
        step = (n + 1) // 2
        return (z + step) % NZ if n % 2 else (z - step + NZ) % NZ

    def w_step(p, *which):
        next(w_rings[p][0], None)
        for n in which if p < 3 else ():
            gate_up_part = w_part(w_place(n), c, 512, 256, 2 * p, 2)
            arrive(gate_up_part, mirror_sid + 8 * p + n)
            push(gate_up_part, gate_up_part, w_core_sid + 8 * p + n, sibling)

    arrive(w_part(z, c, 384, 128), over_sid)
    arrive(w_part(z, c, 512, 256, 6, 2), over_sid + 1)
    for p in range(4):
        w_step(p)
    for dz in (1, 3, 4):
        arrive(values_far.at[dz - 1], far_sid + dz)
    for dz in range(BACK):
        for k in range(1, 4):
            peer = (y_lo + 4 - k) % 4
            arrive_if(key_wanted(dz, peer, y_lo), keys_all.at[dz, peer], key_sid + 4 * dz + k)

    for k in range(1, 8):
        arrive(q_all.at[(head + 8 - k) % 8], q_sid + k)
    place = outer * 512 + y_lo * 128 + lax.broadcasted_iota(jnp.int32, (128, 1), 0)
    start = jnp.zeros((128, 1), jnp.int32)
    bound = jnp.int32(0)
    for j in range(DOCS):
        bound = bound + docs_ref[j]
        start = jnp.where(bound <= place, bound, start)
    for dz in range(BACK):
        keys = keys_all[dz].reshape(512, 128)
        key_place = (outer - dz) * 512 + lax.broadcasted_iota(jnp.int32, (1, 512), 1)
        bias = jnp.where((key_place <= place) & (key_place >= start), 0.0, -1e30)
        for g in range(4):
            heads_q = q_all[:, :, g * 128:(g + 1) * 128].reshape(128, 128)
            scores[g, :, dz * 512:(dz + 1) * 512] = nt(heads_q, keys) * SCALE + bias
    for g in range(4):
        s = scores[g]
        e = jnp.exp(s - jnp.max(s, axis=1, keepdims=True))
        total = jnp.sum(e, axis=1, keepdims=True)
        e = e.astype(BF)
        summed = jnp.zeros((128, 128), F32)
        for dz in range(BACK):
            values = (values_near[pl.ds(y_hi * 4, 4)] if dz == 0 else values_far[dz - 1]).reshape(512, 128)
            summed += jnp.dot(e[:, dz * 512:(dz + 1) * 512], values, preferred_element_type=F32)
        ctx_ref[:, g * 128:(g + 1) * 128] = (summed / total).astype(BF)

    def half_rows(i):
        return ctx_ref.at[pl.ds(pl.multiple_of(i * 64, 64), 64)]

    def ctx_part(i, core):
        return ctx_all.at[i, :, lanes(core, 512)]

    ctx_sid, cross_sid = new(4), new(4)
    for k in range(1, 4):
        peer = (y_lo + k) % 4
        push(half_rows(c), ctx_part(y_lo, c), ctx_sid + k, to_lo(peer))
        push(half_rows(other), ctx_part(y_lo, c), cross_sid + k, to_cross(peer))
    push(half_rows(other), ctx_part(y_lo, c), cross_sid, sibling)
    ctx_all[y_lo, :, lanes(c, 512)] = half_rows(c)[...]

    w_step(0, 0)
    w_step(1, 0)

    proj_sid = new(4)

    def proj_push(i):
        way = (i + NX - x) % NX
        return remote(proj.at[i], proj_in.at[way], proj_sid + way, to_x(i))

    finish(wo_ring)
    wo_wait()
    for k in range(4):
        i = (y_lo + 4 - k) % 4
        if k > 0:
            arrive(ctx_part(i, c), ctx_sid + k)
        arrive(ctx_part(i, other), cross_sid + k)
        proj[i] = nt(ctx_all[i], wo_all[...].reshape(1024, 1024)).astype(BF)

        @pl.when(i != x)
        def _(i=i):
            proj_push(i).start()

        if k in (1, 2):
            w_step(k + 1, 0)

    res_copy.wait()
    total = proj[x].astype(F32)
    for k in range(1, NX):
        arrive(proj_in.at[k], proj_sid + k)
        total += proj_in[k].astype(F32)
    total = (res[...].astype(F32) + total).astype(BF)
    for b in range(2):
        hid[y_lo, b, y_hi, u] = total[:, b * 512:(b + 1) * 512]
    def hid_part(i, b, p, half=None):
        part = hid.at[i % 4, b, i // 4, p]
        return part if half is None else part.at[pl.ds(half * 32, 32)]

    first_sid, second_sid = new(), new(8)
    to_pair = to_x(pair)

    def along_x(i, n):
        push(hid_part(i, 1, u), hid_part(i, 1, u), second_sid + n, to_pair)

    push(hid_part(y, 0, u), hid_part(y, 0, u), first_sid, to_pair)
    y_first = ring(
        NY, y, to_y, lambda i: hid_part(i, 1, u),
        lambda i, b: hid_part(i, 1, u, b), along_x,
    )
    next(y_first)
    w_step(0, 1, 2)
    w_step(1, 1, 2)
    arrive(hid_part(y, 0, 1 - u), first_sid)
    x_first = [
        ring(
            NY, y, to_y, lambda i, p=p: hid_part(i, 0, p),
            lambda i, b, p=p: hid_part(i, 0, p, b),
        )
        for p in range(2)
    ]
    for s in range(4):
        next(x_first[0])
        next(x_first[1])
        next(y_first, None)
        if s == 0:
            w_step(2, 1, 2)
            w_step(3, 1, 2)
        if s in (1, 2):
            w_step(2 * s - 2, 3, 4)
            w_step(2 * s - 1, 3, 4)
        if s == 3:
            w_step(0, 5, 6)
            w_step(1, 5, 6)
    for gen in x_first:
        next(gen, None)
    for n in range(8):
        step = (n + 1) // 2
        i = (y + step) % NY if n % 2 else (y - step + NY) % NY
        arrive(hid_part(i, 1, 1 - u), second_sid + n)
    for k in range(1, 4):
        arrive(gains.at[(y_lo + 4 - k) % 4], gain_sid + k)
    w_step(2, 5, 6)
    w_step(3, 5, 6)
    for p in range(4):
        w_step(p, 7)
        w_rings[p][1]()
        for n in range(8 if p < 3 else 0):
            arrive(w_part(w_place(n), other, 512, 256, 2 * p, 2), w_core_sid + 8 * p + n)

    acc[...] = jnp.zeros_like(acc)

    def gate_up(f, squares):
        gain_row = gains[f // 2]
        rows = hid[f // 2, f % 2].reshape(256, 512).astype(F32)
        scaled = jnp.concatenate(
            [
                rows[:, j * 128:(j + 1) * 128]
                * jnp.where(f % 2 == 0, gain_row[j:j + 1], gain_row[4 + j:5 + j])
                for j in range(4)
            ],
            axis=1,
        ).astype(BF)
        for s, first in enumerate(SLOTS):
            weights = w_all[f, :, :, first:first + 256].reshape(512, 256)
            acc[s] += jnp.dot(scaled, weights, preferred_element_type=F32)
        return squares + jnp.sum(rows * rows, axis=1, keepdims=True)

    squares = lax.fori_loop(0, 8, gate_up, jnp.zeros((256, 1), F32))
    inverse = lax.rsqrt(squares / D + 1e-05)
    for s in range(4):
        gate, up = acc[s, :, :128] * inverse, acc[s, :, 128:] * inverse
        act[:, s * 128:(s + 1) * 128] = (gate / (1.0 + jnp.exp(-gate)) * up).astype(BF)

    x_sid, odd_sid = new(4), new()

    def project_down(lo, b):
        f = lo * 2 + b
        weights = jnp.concatenate(
            [w_all[f, :, :, s * 768 + 256:s * 768 + 512].reshape(512, 256) for s in range(2)], axis=1
        )
        down[lo, b] = nt(act[...], weights).astype(BF).reshape(2, 2, 64, 512)

    def sum_ring(block, slots):
        sid = new(8)
        to_way = to_y((y + 1) % NY), to_y((y + NY - 1) % NY)

        def run():
            for s in range(4):
                for way in range(2):
                    buf, first_sid = slots.at[way], sid + 4 * way
                    i = (y + 4 - s) % NY if way == 0 else (y + 4 + s) % NY
                    half = pl.ds(32 * way, 32)
                    if s == 0:
                        push(block(i, 32 * way, 32), buf.at[0, half], first_sid, to_way[way])
                        continue
                    if s == 1:
                        arrive(buf.at[0, half], first_sid)
                        mine = block(i, 32 * way, 32)[...]
                        buf[0, half] = (buf[0, half].astype(F32) + mine.astype(F32)).astype(BF)
                        buf[0, pl.ds(32 * (1 - way), 32)] = block(i, 32 * (1 - way), 32)[...]
                    else:
                        arrive(buf.at[s - 1], first_sid + s - 1)
                        mine = block(i, 0, 64)[...]
                        buf[s - 1] = (buf[s - 1].astype(F32) + mine.astype(F32)).astype(BF)
                    push(buf.at[s - 1], buf.at[s], first_sid + s, to_way[way])
                yield

        def total():
            result = block(y, 0, 64)[...].astype(F32)
            for way in range(2):
                arrive(slots.at[way, 3], sid + 4 * way + 3)
                result += slots[way, 3].astype(F32)
            return result

        return run(), total

    odd_rings = [
        sum_ring(
            lambda i, first, count, p=p: down.at[i % 4, 1, i // 4, p, pl.ds(first, count)], rings.at[p]
        )
        for p in range(2)
    ]
    even_ring = sum_ring(lambda i, first, count: x_sum.at[i % 4, i // 4, pl.ds(first, count)], rings.at[2])

    def odd_step():
        for gen, _ in odd_rings:
            next(gen)

    def add_even(*pieces):
        for k in pieces:
            lo = (y_lo + k) % 4
            arrive(x_in.at[k], x_sid + k)
            for g in range(2):
                x_sum[lo, g] = (down[lo, 0, g, u].astype(F32) + x_in[k, g].astype(F32)).astype(BF)
        next(even_ring[0])

    for k in (0, 1, 3, 2):
        lo = (y_lo + k) % 4
        project_down(lo, 0)
        push(down.at[lo, 0, :, 1 - u], x_in.at[k], x_sid + k, to_pair)
    for k in (0, 1, 3, 2):
        project_down((y_lo + k) % 4, 1)
        if k == 0:
            odd_step()

    add_even(0)
    odd_step()
    add_even(1, 3)
    odd_step()
    add_even(2)
    odd_step()
    add_even()
    for p in range(2):
        odd_sum[p] = odd_rings[p][1]().astype(BF)
    push(odd_sum.at[1 - u], odd_in, odd_sid, to_pair)
    out_ref[:, :512] = (hid[y_lo, 0, y_hi, u].astype(F32) + even_ring[1]()).astype(BF)
    arrive(odd_in, odd_sid)
    total = odd_sum[u].astype(F32) + odd_in[...].astype(F32)
    out_ref[:, 512:] = (hid[y_lo, 1, y_hi, u].astype(F32) + total).astype(BF)

    for copy in sends:
        copy.wait_send()
    for cond, args in maybes:
        @pl.when(cond)
        def _(args=args):
            remote(*args).wait_send()

    for i in range(NX):
        @pl.when(i != x)
        def _(i=i):
            proj_push(i).wait_send()

    for k in range(1, NY):
        peer = (y + k) % NY

        @pl.when(peer != NY - 1)
        def _(k=k, peer=peer):
            for part, src in enumerate(w_sources(peer)):
                remote(
                    src, w_all.at[feat(y), z, :, w_cols(part, c)], w_sid + 3 * k + part, to_y(peer)
                ).wait_send()

    assert counter[0] <= SEMS, counter[0]


SEMS = 460
SLOTS = (0, 512, 768, 1280)


def per_device(query, key, value, doc_lengths, resid, norm_gain, w_out, w_gate_up, w_down):
    vmem = pl.BlockSpec(memory_space=pltpu.VMEM)
    anywhere = pl.BlockSpec(memory_space=pl.ANY)
    smem = pl.BlockSpec(memory_space=pltpu.SMEM)

    def buf(*shape, kind=BF):
        return pltpu.VMEM(shape, kind)

    return pl.pallas_call(
        kernel,
        out_shape=(
            jax.ShapeDtypeStruct((128, 512), BF),
            jax.ShapeDtypeStruct((64, 1024), BF),
        ),
        in_specs=[anywhere, anywhere, anywhere, smem, anywhere, vmem, anywhere, anywhere, anywhere],
        out_specs=(vmem, vmem),
        scratch_shapes=[
            buf(8, 16, 512),
            buf(BACK, 4, 8, 16, 128),
            buf(8, 8, 16, 128),
            buf(BACK - 1, 4, 8, 16, 128),
            buf(4, 8, 16, 128),
            buf(4, 128, BACK * 512, kind=F32),
            buf(4, 64, 1024),
            buf(2, 8, 64, 1024),
            buf(8, 8, 64, 1536),
            buf(64, 1024),
            buf(4, 8, 128, kind=F32),
            buf(4, 64, 1024),
            buf(4, 64, 1024),
            buf(4, 2, 2, 2, 64, 512),
            buf(4, 256, 256, kind=F32),
            buf(256, 512),
            buf(4, 2, 2, 2, 64, 512),
            buf(4, 2, 64, 512),
            buf(4, 2, 64, 512),
            buf(3, 2, 4, 64, 512),
            buf(2, 64, 512),
            buf(64, 512),
            pltpu.SemaphoreType.DMA((SEMS,)),
            pltpu.SemaphoreType.DMA((SEMS,)),
            pltpu.SemaphoreType.DMA((16,)),
        ],
        compiler_params=pltpu.CompilerParams(
            collective_id=0, has_side_effects=True, vmem_limit_bytes=56 * 1024 * 1024
        ),
        cost_estimate=pl.CostEstimate(flops=4_000_000_000, bytes_accessed=4_000_000, transcendentals=2_000_000),
    )(
        query, key, value, doc_lengths, resid, norm_gain.reshape(8, 128),
        w_out.T, w_gate_up, w_down.T,
    )


def solution(mesh):
    placed = (
        P(("outer", "inner", "head"), None),
        P(("outer", "inner", "head"), None),
        P(("outer", "inner", "head"), None),
        P(),
        P("outer", "inner"),
        P("inner"),
        P("head", ("inner", "outer")),
        P(None, ("inner", "outer"), "head"),
        P("head", ("inner", "outer")),
    )
    return jax.shard_map(
        per_device,
        mesh=mesh,
        in_specs=placed,
        out_specs=(P(("outer", "inner"), "head"), P(("outer", "head"), "inner")),
        check_vma=False,
    )
```

```python
import math

import jax
import jax.numpy as jnp
from jax import lax
from jax.experimental import pallas as pl
from jax.experimental.pallas import tpu as pltpu
from jax.sharding import PartitionSpec as P

MESH = pl.DeviceIdType.MESH
D = 4096
BF = jnp.bfloat16
F32 = jnp.float32
SCALE = 128 ** (-0.5)
DOCS = 24
NX, NY, NZ = 4, 8, 8
BACK = 5


def nt(a, b):
    return lax.dot_general(a, b, (((1,), (1,)), ((), ())), preferred_element_type=F32)


def kernel(
    q_ref, k_ref, v_ref, docs_ref, resid_ref, gain_ref, wo_ref, wgu_ref, wd_ref,
    ctx_ref, out_ref,
    q_all, keys_all, values_near, values_far, relay, scores, ctx_own, ctx_all, wo_all, w_all, res, gains,
    proj, proj_in, hid, acc, act, down, x_in, x_sum, rings, odd_sum, odd_in,
    send_sem, recv_sem, local_sem,
):
    head = lax.axis_index("head")
    y_lo = lax.axis_index("inner")
    outer = lax.axis_index("outer")
    x, c = head // 2, head % 2
    u, pair, mirror = x % 2, x + 1 - 2 * (x % 2), 3 - x
    y_hi, z = outer // NZ, outer % NZ
    y = y_hi * 4 + y_lo
    other = 1 - c

    def to_head(h):
        return {"head": h}

    def to_x(i):
        return {"head": i * 2 + c}

    def to_y(i):
        return {"inner": i % 4, "outer": (i // 4) * NZ + z}

    def to_z(i):
        return {"outer": y_hi * NZ + i}

    def to_outer(i):
        return {"outer": i}

    def to_lo(i):
        return {"inner": i}

    def to_cross(i):
        return {"head": x * 2 + other, "inner": i}

    sibling = to_head(x * 2 + other)

    def feat(i):
        return (i % 4) * 2 + i // 4

    counter = [0]

    def new(count=1):
        counter[0] += count
        return counter[0] - count

    def remote(src, dst, sid, dev, ssid=0):
        return pltpu.make_async_remote_copy(
            src_ref=src, dst_ref=dst, send_sem=send_sem.at[ssid], recv_sem=recv_sem.at[sid],
            device_id=dev, device_id_type=MESH,
        )

    sent = [0]

    def count(units):
        sent[-1] += units
        if sent[-1] >= FULL and block_shape(sent[-1]) is not None:
            sent.append(0)

    def push(src, dst, sid, dev):
        remote(src, dst, sid, dev, len(sent) - 1).start()
        count(math.prod(src.shape) * jnp.dtype(src.dtype).itemsize // 4096)

    maybes = []

    def push_if(cond, src, dst, sid, dev):
        copy = (src, dst, sid, dev, SHARED + 1 + len(maybes))

        @pl.when(cond)
        def _():
            remote(*copy).start()

        maybes.append((cond, copy))

    def arrive_if(cond, *args):
        @pl.when(cond)
        def _():
            arrive(*args)

    def arrive(dst, sid):
        remote(dst, dst, sid, sibling).wait_recv()

    local_count = [0]

    def local(src, dst, sem=None):
        if sem is None:
            sem = local_sem.at[local_count[0]]
            local_count[0] += 1
        copy = pltpu.make_async_copy(src, dst, sem)
        copy.start()
        return copy

    def ring(n, me, to, chunk, half, arrived=None):
        steps = n // 2
        sr, sl = new(steps), new(steps)
        right, left = to((me + 1) % n), to((me + n - 1) % n)

        def run():
            for s in range(steps):
                back, ahead = (me - s + n) % n, (me + s) % n
                if s > 0:
                    arrive(chunk(back), sr + s - 1)
                    arrive(chunk(ahead), sl + s - 1)
                if s < steps - 1:
                    push(chunk(back), chunk(back), sr + s, right)
                    push(chunk(ahead), chunk(ahead), sl + s, left)
                elif half is None:
                    push(chunk(ahead), chunk(ahead), sl + s, left)
                else:
                    push(half(back, 0), half(back, 0), sr + s, right)
                    push(half(ahead, 1), half(ahead, 1), sl + s, left)
                if arrived is not None:
                    arrived(back, 2 * s)
                    if s > 0:
                        arrived(ahead, 2 * s - 1)
                yield
            far = (me + steps) % n
            if half is None:
                arrive(chunk(far), sl + steps - 1)
            else:
                arrive(half(far, 0), sr + steps - 1)
                arrive(half(far, 1), sl + steps - 1)
            if arrived is not None:
                arrived(far, 2 * steps - 1)

        return run()

    def finish(gen):
        for _ in gen:
            pass

    def together(gens):
        for _ in range(5):
            for gen in gens:
                next(gen, None)

    def lanes(core, width):
        return pl.ds(pl.multiple_of(core * width, width), width)

    keys_all[...] = jnp.zeros_like(keys_all)
    values_near[...] = jnp.zeros_like(values_near)

    barrier = pltpu.get_barrier_semaphore()
    for k in range(1, 8):
        pl.semaphore_signal(barrier, inc=1, device_id=to_head((head + k) % 8), device_id_type=MESH)
        pl.semaphore_signal(barrier, inc=1, device_id=to_y((y + k) % NY), device_id_type=MESH)
    for k in range(1, BACK):
        for peer in ((outer + k) % 16, (outer + 16 - k) % 16):
            pl.semaphore_signal(barrier, inc=1, device_id=to_outer(peer), device_id_type=MESH)
        pl.semaphore_signal(barrier, inc=1, device_id=to_z((z + k) % NZ), device_id_type=MESH)
        pl.semaphore_signal(barrier, inc=1, device_id=to_z((z + NZ - k) % NZ), device_id_type=MESH)
    for k in range(1, 4):
        pl.semaphore_signal(barrier, inc=1, device_id=to_cross((y_lo + k) % 4), device_id_type=MESH)
    pl.semaphore_wait(barrier, 33)

    k_sid, v_sid, q_sid = new(), new(), new()
    for k in range(1, 8):
        peer = (head + k) % 8
        cols = pl.ds(pl.multiple_of(peer * 128, 128), 128)
        push(k_ref.at[:, cols], keys_all.at[0, y_lo, head], k_sid, to_head(peer))
        push(v_ref.at[:, cols], values_near.at[y, head], v_sid, to_head(peer))
    own = pl.ds(pl.multiple_of(head * 128, 128), 128)
    local(k_ref.at[:, own], keys_all.at[0, y_lo, head], recv_sem.at[k_sid])
    local(v_ref.at[:, own], values_near.at[y, head], recv_sem.at[v_sid])
    for k in range(1, 8):
        peer = (head + k) % 8
        cols = pl.ds(pl.multiple_of(peer * 512, 512), 512)
        push(q_ref.at[:, cols], q_all.at[head], q_sid, to_head(peer))
    local(q_ref.at[:, pl.ds(pl.multiple_of(head * 512, 512), 512)], q_all.at[head], recv_sem.at[q_sid])

    w_sid = new()

    def w_cols(part, s):
        return pl.ds(pl.multiple_of(s * 768 + part * 128, 128), 128)

    def w_sources(i):
        cols = pl.ds(pl.multiple_of(i * 128, 128), 128)
        return wgu_ref.at[0, :, cols], wgu_ref.at[1, :, cols], wd_ref.at[:, cols]

    def w_exchange(parts):
        for k in range(1, NY):
            peer = (y + k) % NY

            @pl.when(peer != NY - 1)
            def _(k=k, peer=peer):
                for part in parts:
                    remote(
                        w_sources(peer)[part], w_all.at[feat(y), z, :, w_cols(part, c)],
                        w_sid, to_y(peer), SHARED,
                    ).start()

    def w_exchanged():
        @pl.when(y != NY - 1)
        def _():
            arrive(w_part(z, c, 0, 384), w_sid)

    @pl.when(y != NY - 1)
    def _():
        for part, src in enumerate(w_sources(y)):
            pltpu.make_async_copy(
                src, w_all.at[feat(y), z, :, w_cols(part, c)], recv_sem.at[w_sid]
            ).start()

    @pl.when(y == NY - 1)
    def _():
        def zero(f, _):
            w_all[f, z, :, pl.ds(pl.multiple_of(c * 768, 128), 384)] = jnp.zeros((64, 384), BF)
            return 0

        lax.fori_loop(0, 8, zero, 0)

    wo_sid = new()
    push(wo_ref, wo_all.at[y_hi, z, :, lanes(c, 512)], wo_sid, to_y((1 - y_hi) * 4 + y_lo))
    wo_copy = local(wo_ref, wo_all.at[y_hi, z, :, lanes(c, 512)])
    res_copy = local(resid_ref.at[pl.ds(pl.multiple_of(head * 64, 64), 64)], res)

    arrive(keys_all.at[0, y_lo], k_sid)
    arrive(values_near.at[y], v_sid)

    def shared_ring(buf_chunk, sid, then=None, buf_half=None):
        def arrived(i, n):
            push(buf_chunk(i, c), buf_chunk(i, c), sid, sibling)
            if then is not None:
                then(i, n)

        half = None if buf_half is None else lambda i, b: buf_half(i, b, c)
        return ring(NZ, z, to_z, lambda i: buf_chunk(i, c), half, arrived)

    wo_core_sid = new()
    wo_ring = shared_ring(lambda i, s: wo_all.at[:, i, :, lanes(s, 512)], wo_core_sid)

    ahead_sid, key_sid, near_sid, far_sid = new(BACK), new(4 * BACK), new(8), new(BACK + 1)

    def key_wanted(dz, src, dst):
        seen = outer >= dz
        return seen & (src < dst) if dz == 0 else seen & (src > dst) if dz == 4 else seen

    def key_lo(dz):
        for k in range(1, 4):
            peer = (y_lo + k) % 4
            push_if(
                key_wanted(dz, y_lo, peer),
                keys_all.at[dz, y_lo], keys_all.at[dz, y_lo], key_sid + 4 * dz + k, to_lo(peer),
            )

    def key_ahead(dz):
        arrive_if(outer >= dz, keys_all.at[dz, y_lo], ahead_sid + dz)

    def near_wanted(row):
        return (row == y_hi) | ((z >= 4) & (row == 0))

    for k in range(1, NY):
        peer = (y + k) % NY
        push_if(
            (peer // 4 == y_hi) | ((z >= 4) & (y_hi == 0)),
            values_near.at[y], values_near.at[y], near_sid + k, to_y(peer),
        )
    for dz in range(1, BACK):
        push_if(
            outer + dz < 16,
            keys_all.at[0, y_lo], keys_all.at[dz, y_lo], ahead_sid + dz, to_outer((outer + dz) % 16),
        )
    key_lo(0)
    wo_copy.wait()
    arrive(wo_all.at[1 - y_hi, z, :, lanes(c, 512)], wo_sid)
    next(wo_ring)
    for k in range(1, NY):
        peer = (y + NY - k) % NY
        arrive_if(near_wanted(peer // 4), values_near.at[peer], near_sid + k)
        if k == 4:
            next(wo_ring)

    def row_blocks(dz):
        return values_near.at[pl.ds(jnp.where(z + dz < NZ, y_hi, 1 - y_hi) * 4, 4)]

    push(row_blocks(4), relay, far_sid, to_z((z + NZ - 2) % NZ))
    for dz in range(1, 3):
        push(row_blocks(dz), values_far.at[dz - 1], far_sid + dz, to_z((z + dz) % NZ))
    push_if(z == NZ - 3, row_blocks(3), values_far.at[2], far_sid + 3, to_z((z + 3) % NZ))
    w_exchange([0, 1, 2])
    for dz in range(1, 3):
        key_ahead(dz)
        key_lo(dz)
    next(wo_ring)
    arrive(values_far.at[1], far_sid + 2)
    push_if(z != NZ - 1, values_far.at[1], values_far.at[2], far_sid + 3, to_z((z + 1) % NZ))
    arrive(relay, far_sid)
    push(relay, values_far.at[3], far_sid + 4, to_z((z + NZ - 2) % NZ))
    for dz in range(3, BACK):
        key_ahead(dz)
        key_lo(dz)

    def w_part(i, s, first, width, f=0, count=8):
        return w_all.at[pl.ds(f, count), i, :, pl.ds(pl.multiple_of(s * 768 + first, 128), width)]

    over_sid, mirror_sid, w_core_sid = new(2), new(24), new()
    to_mirror = to_x(mirror)
    next(wo_ring)
    gain_sid = new(4)
    for k in range(1, 4):
        push(gain_ref, gains.at[y_lo], gain_sid + k, to_lo((y_lo + k) % 4))
    gains[y_lo] = gain_ref[...]
    w_exchanged()
    push(w_part(z, c, 256, 128), w_part(z, c, 384, 128), over_sid, to_mirror)
    push(w_part(z, c, 0, 256, 6, 2), w_part(z, c, 512, 256, 6, 2), over_sid + 1, to_mirror)

    def w_quarter_ring(p):
        if p == 3:
            return shared_ring(
                lambda i, s: w_part(i, s, 0, 768, 6, 2), w_core_sid, None,
                lambda i, b, s: w_part(i, s, 0, 768, 6 + b, 1),
            )

        def w_arrived(i, n):
            push(
                w_part(i, c, 0, 256, 2 * p, 2), w_part(i, c, 512, 256, 2 * p, 2),
                mirror_sid + 8 * p + n, to_mirror,
            )

        return shared_ring(
            lambda i, s: w_part(i, s, 0, 512, 2 * p, 2), w_core_sid, w_arrived,
            lambda i, b, s: w_part(i, s, 0, 512, 2 * p + b, 1),
        )

    w_rings = [w_quarter_ring(p) for p in range(4)]

    def w_place(n):
        step = (n + 1) // 2
        return (z + step) % NZ if n % 2 else (z - step + NZ) % NZ

    def w_step(p, *which):
        next(w_rings[p], None)
        for n in which if p < 3 else ():
            gate_up_part = w_part(w_place(n), c, 512, 256, 2 * p, 2)
            arrive(gate_up_part, mirror_sid + 8 * p + n)
            push(gate_up_part, gate_up_part, w_core_sid, sibling)

    arrive(w_part(z, c, 384, 128), over_sid)
    arrive(w_part(z, c, 512, 256, 6, 2), over_sid + 1)
    for p in range(4):
        w_step(p)
    for dz in (1, 3, 4):
        arrive(values_far.at[dz - 1], far_sid + dz)
    for dz in range(BACK):
        for k in range(1, 4):
            peer = (y_lo + 4 - k) % 4
            arrive_if(key_wanted(dz, peer, y_lo), keys_all.at[dz, peer], key_sid + 4 * dz + k)

    arrive(q_all, q_sid)
    place = outer * 512 + y_lo * 128 + lax.broadcasted_iota(jnp.int32, (128, 1), 0)
    start = jnp.zeros((128, 1), jnp.int32)
    bound = jnp.int32(0)
    for j in range(DOCS):
        bound = bound + docs_ref[j]
        start = jnp.where(bound <= place, bound, start)
    for dz in range(BACK):
        keys = keys_all[dz].reshape(512, 128)
        key_place = (outer - dz) * 512 + lax.broadcasted_iota(jnp.int32, (1, 512), 1)
        bias = jnp.where((key_place <= place) & (key_place >= start), 0.0, -1e30)
        for g in range(4):
            heads_q = q_all[:, :, g * 128:(g + 1) * 128].reshape(128, 128)
            scores[g, :, dz * 512:(dz + 1) * 512] = nt(heads_q, keys) * SCALE + bias
    for g in range(4):
        s = scores[g]
        e = jnp.exp(s - jnp.max(s, axis=1, keepdims=True))
        total = jnp.sum(e, axis=1, keepdims=True)
        e = e.astype(BF)
        summed = jnp.zeros((128, 128), F32)
        for dz in range(BACK):
            values = (values_near[pl.ds(y_hi * 4, 4)] if dz == 0 else values_far[dz - 1]).reshape(512, 128)
            summed += jnp.dot(e[:, dz * 512:(dz + 1) * 512], values, preferred_element_type=F32)
        ctx_own[:, g * 128:(g + 1) * 128] = (summed / total).astype(BF)

    def half_rows(i):
        return ctx_own.at[pl.ds(pl.multiple_of(i * 64, 64), 64)]

    ctx_copy = local(ctx_own, ctx_ref)

    def ctx_part(i, core):
        return ctx_all.at[i, :, lanes(core, 512)]

    ctx_sid, cross_sid = new(4), new(4)
    for k in range(1, 4):
        peer = (y_lo + k) % 4
        push(half_rows(c), ctx_part(y_lo, c), ctx_sid + k, to_lo(peer))
        push(half_rows(other), ctx_part(y_lo, c), cross_sid + k, to_cross(peer))
    push(half_rows(other), ctx_part(y_lo, c), cross_sid, sibling)
    ctx_all[y_lo, :, lanes(c, 512)] = half_rows(c)[...]

    w_step(0, 0)
    w_step(1, 0)

    proj_sid = new(4)

    def proj_push(i):
        way = (i + NX - x) % NX
        return remote(proj.at[i], proj_in.at[way], proj_sid + way, to_x(i), PROJ)

    finish(wo_ring)
    arrive(wo_all.at[:, :, :, lanes(other, 512)], wo_core_sid)
    for k in range(4):
        i = (y_lo + 4 - k) % 4
        if k > 0:
            arrive(ctx_part(i, c), ctx_sid + k)
        arrive(ctx_part(i, other), cross_sid + k)
        proj[i] = nt(ctx_all[i], wo_all[...].reshape(1024, 1024)).astype(BF)

        @pl.when(i != x)
        def _(i=i):
            proj_push(i).start()

        if k in (1, 2):
            w_step(k + 1, 0)

    res_copy.wait()
    total = proj[x].astype(F32)
    for k in range(1, NX):
        arrive(proj_in.at[k], proj_sid + k)
        total += proj_in[k].astype(F32)
    total = (res[...].astype(F32) + total).astype(BF)
    for b in range(2):
        hid[y_lo, b, y_hi, u] = total[:, b * 512:(b + 1) * 512]
    def hid_part(i, b, p, half=None):
        part = hid.at[i % 4, b, i // 4, p]
        return part if half is None else part.at[pl.ds(half * 32, 32)]

    first_sid, second_sid = new(), new()
    to_pair = to_x(pair)

    def along_x(i, n):
        push(hid_part(i, 1, u), hid_part(i, 1, u), second_sid, to_pair)

    push(hid_part(y, 0, u), hid_part(y, 0, u), first_sid, to_pair)
    y_first = ring(
        NY, y, to_y, lambda i: hid_part(i, 1, u),
        lambda i, b: hid_part(i, 1, u, b), along_x,
    )
    next(y_first)
    w_step(0, 1, 2)
    w_step(1, 1, 2)
    arrive(hid_part(y, 0, 1 - u), first_sid)
    x_first = [
        ring(
            NY, y, to_y, lambda i, p=p: hid_part(i, 0, p),
            lambda i, b, p=p: hid_part(i, 0, p, b),
        )
        for p in range(2)
    ]
    for s in range(4):
        next(x_first[0])
        next(x_first[1])
        next(y_first, None)
        if s == 0:
            w_step(2, 1, 2)
            w_step(3, 1, 2)
        if s in (1, 2):
            w_step(2 * s - 2, 3, 4)
            w_step(2 * s - 1, 3, 4)
        if s == 3:
            w_step(0, 5, 6)
            w_step(1, 5, 6)
    for gen in x_first:
        next(gen, None)
    arrive(hid.at[:, 1, :, 1 - u], second_sid)
    for k in range(1, 4):
        arrive(gains.at[(y_lo + 4 - k) % 4], gain_sid + k)
    w_step(2, 5, 6)
    w_step(3, 5, 6)
    for p in range(4):
        w_step(p, 7)
    arrive(w_all.at[:, :, :, lanes(other, 768)], w_core_sid)

    acc[...] = jnp.zeros_like(acc)

    def gate_up(f, squares):
        gain_row = gains[f // 2]
        rows = hid[f // 2, f % 2].reshape(256, 512).astype(F32)
        scaled = jnp.concatenate(
            [
                rows[:, j * 128:(j + 1) * 128]
                * jnp.where(f % 2 == 0, gain_row[j:j + 1], gain_row[4 + j:5 + j])
                for j in range(4)
            ],
            axis=1,
        ).astype(BF)
        for s, first in enumerate(SLOTS):
            weights = w_all[f, :, :, first:first + 256].reshape(512, 256)
            acc[s] += jnp.dot(scaled, weights, preferred_element_type=F32)
        return squares + jnp.sum(rows * rows, axis=1, keepdims=True)

    squares = lax.fori_loop(0, 8, gate_up, jnp.zeros((256, 1), F32))
    inverse = lax.rsqrt(squares / D + 1e-05)
    for s in range(4):
        gate, up = acc[s, :, :128] * inverse, acc[s, :, 128:] * inverse
        act[:, s * 128:(s + 1) * 128] = (gate / (1.0 + jnp.exp(-gate)) * up).astype(BF)

    x_sid, odd_sid = new(4), new()

    def project_down(lo, b):
        f = lo * 2 + b
        weights = jnp.concatenate(
            [w_all[f, :, :, s * 768 + 256:s * 768 + 512].reshape(512, 256) for s in range(2)], axis=1
        )
        down[lo, b] = nt(act[...], weights).astype(BF).reshape(2, 2, 64, 512)

    def sum_ring(block, slots):
        sid = new(8)
        to_way = to_y((y + 1) % NY), to_y((y + NY - 1) % NY)

        def run():
            for s in range(4):
                for way in range(2):
                    buf, first_sid = slots.at[way], sid + 4 * way
                    i = (y + 4 - s) % NY if way == 0 else (y + 4 + s) % NY
                    half = pl.ds(32 * way, 32)
                    if s == 0:
                        push(block(i, 32 * way, 32), buf.at[0, half], first_sid, to_way[way])
                        continue
                    if s == 1:
                        arrive(buf.at[0, half], first_sid)
                        mine = block(i, 32 * way, 32)[...]
                        buf[0, half] = (buf[0, half].astype(F32) + mine.astype(F32)).astype(BF)
                        buf[0, pl.ds(32 * (1 - way), 32)] = block(i, 32 * (1 - way), 32)[...]
                    else:
                        arrive(buf.at[s - 1], first_sid + s - 1)
                        mine = block(i, 0, 64)[...]
                        buf[s - 1] = (buf[s - 1].astype(F32) + mine.astype(F32)).astype(BF)
                    push(buf.at[s - 1], buf.at[s], first_sid + s, to_way[way])
                yield

        def total():
            result = block(y, 0, 64)[...].astype(F32)
            for way in range(2):
                arrive(slots.at[way, 3], sid + 4 * way + 3)
                result += slots[way, 3].astype(F32)
            return result

        return run(), total

    odd_rings = [
        sum_ring(
            lambda i, first, count, p=p: down.at[i % 4, 1, i // 4, p, pl.ds(first, count)], rings.at[p]
        )
        for p in range(2)
    ]
    even_ring = sum_ring(lambda i, first, count: x_sum.at[i % 4, i // 4, pl.ds(first, count)], rings.at[2])

    def odd_step():
        for gen, _ in odd_rings:
            next(gen)

    def add_even(*pieces):
        for k in pieces:
            lo = (y_lo + k) % 4
            arrive(x_in.at[k], x_sid + k)
            for g in range(2):
                x_sum[lo, g] = (down[lo, 0, g, u].astype(F32) + x_in[k, g].astype(F32)).astype(BF)
        next(even_ring[0])

    for k in (0, 1, 3, 2):
        lo = (y_lo + k) % 4
        project_down(lo, 0)
        push(down.at[lo, 0, :, 1 - u], x_in.at[k], x_sid + k, to_pair)
    for k in (0, 1, 3, 2):
        project_down((y_lo + k) % 4, 1)
        if k == 0:
            odd_step()

    add_even(0)
    odd_step()
    add_even(1, 3)
    odd_step()
    add_even(2)
    odd_step()
    add_even()
    for p in range(2):
        odd_sum[p] = odd_rings[p][1]().astype(BF)
    push(odd_sum.at[1 - u], odd_in, odd_sid, to_pair)
    out_ref[:, :512] = (hid[y_lo, 0, y_hi, u].astype(F32) + even_ring[1]()).astype(BF)
    arrive(odd_in, odd_sid)
    total = odd_sum[u].astype(F32) + odd_in[...].astype(F32)
    out_ref[:, 512:] = (hid[y_lo, 1, y_hi, u].astype(F32) + total).astype(BF)

    ctx_copy.wait()
    if sent[-1] == 0:
        sent.pop()
    for ssid, units in enumerate(sent):
        block = w_all.at[tuple(pl.ds(0, n) for n in block_shape(units))]
        remote(block, block, 0, sibling, ssid).wait_send()
    for cond, copy in maybes:
        @pl.when(cond)
        def _(copy=copy):
            remote(*copy).wait_send()

    remote(proj.at[pl.ds(0, 3)], proj.at[pl.ds(0, 3)], 0, sibling, PROJ).wait_send()

    for last, count in ((False, 6), (True, 7)):
        @pl.when((y == NY - 1) == last)
        def _(count=count):
            pieces = w_all.at[pl.ds(0, count), 0, :, pl.ds(0, 384)]
            remote(pieces, pieces, 0, sibling, SHARED).wait_send()

    assert counter[0] == RECV and len(sent) == SHARED and local_count[0] == LOCAL, (counter[0], len(sent), sent)
    assert PROJ + 1 == SEND and len(maybes) == MAYBES, len(maybes)


RECV, LOCAL, MAYBES, SHARED, FULL = 183, 3, 28, 17, 253
PROJ = SHARED + 1 + MAYBES
SEND = PROJ + 1


def block_shape(units):
    shapes = (
        (a, b, 16 * r, 128 * t)
        for a in range(1, 9) for b in range(1, 9) for r in range(1, 5) for t in range(1, 13)
        if a * b * r * t == units
    )
    return next(shapes, None)


SLOTS = (0, 512, 768, 1280)


def per_device(query, key, value, doc_lengths, resid, norm_gain, w_out, w_gate_up, w_down):
    vmem = pl.BlockSpec(memory_space=pltpu.VMEM)
    anywhere = pl.BlockSpec(memory_space=pl.ANY)
    smem = pl.BlockSpec(memory_space=pltpu.SMEM)

    def buf(*shape, kind=BF):
        return pltpu.VMEM(shape, kind)

    return pl.pallas_call(
        kernel,
        out_shape=(
            jax.ShapeDtypeStruct((128, 512), BF),
            jax.ShapeDtypeStruct((64, 1024), BF),
        ),
        in_specs=[anywhere, anywhere, anywhere, smem, anywhere, vmem, anywhere, anywhere, anywhere],
        out_specs=(anywhere, vmem),
        scratch_shapes=[
            buf(8, 16, 512),
            buf(BACK, 4, 8, 16, 128),
            buf(8, 8, 16, 128),
            buf(BACK - 1, 4, 8, 16, 128),
            buf(4, 8, 16, 128),
            buf(4, 128, BACK * 512, kind=F32),
            buf(128, 512),
            buf(4, 64, 1024),
            buf(2, 8, 64, 1024),
            buf(8, 8, 64, 1536),
            buf(64, 1024),
            buf(4, 8, 128, kind=F32),
            buf(4, 64, 1024),
            buf(4, 64, 1024),
            buf(4, 2, 2, 2, 64, 512),
            buf(4, 256, 256, kind=F32),
            buf(256, 512),
            buf(4, 2, 2, 2, 64, 512),
            buf(4, 2, 64, 512),
            buf(4, 2, 64, 512),
            buf(3, 2, 4, 64, 512),
            buf(2, 64, 512),
            buf(64, 512),
            pltpu.SemaphoreType.DMA((SEND,)),
            pltpu.SemaphoreType.DMA((RECV,)),
            pltpu.SemaphoreType.DMA((LOCAL,)),
        ],
        compiler_params=pltpu.CompilerParams(
            collective_id=0, has_side_effects=True, vmem_limit_bytes=56 * 1024 * 1024
        ),
        cost_estimate=pl.CostEstimate(flops=4_000_000_000, bytes_accessed=4_000_000, transcendentals=2_000_000),
    )(
        query, key, value, doc_lengths, resid, norm_gain.reshape(8, 128),
        w_out.T, w_gate_up, w_down.T,
    )


def solution(mesh):
    placed = (
        P(("outer", "inner", "head"), None),
        P(("outer", "inner", "head"), None),
        P(("outer", "inner", "head"), None),
        P(),
        P("outer", "inner"),
        P("inner"),
        P("head", ("inner", "outer")),
        P(None, ("inner", "outer"), "head"),
        P("head", ("inner", "outer")),
    )
    return jax.shard_map(
        per_device,
        mesh=mesh,
        in_specs=placed,
        out_specs=(P(("outer", "inner"), "head"), P(("outer", "head"), "inner")),
        check_vma=False,
    )
```

```python
import math

import jax
import jax.numpy as jnp
from jax import lax
from jax.experimental import pallas as pl
from jax.experimental.pallas import tpu as pltpu
from jax.sharding import PartitionSpec as P

MESH = pl.DeviceIdType.MESH
D = 4096
BF = jnp.bfloat16
F32 = jnp.float32
SCALE = 128 ** (-0.5)
DOCS = 24
NX, NY, NZ = 4, 8, 8
BACK = 5


def nt(a, b):
    return lax.dot_general(a, b, (((1,), (1,)), ((), ())), preferred_element_type=F32)


def kernel(
    q_ref, k_ref, v_ref, docs_ref, resid_ref, gain_ref, wo_ref, wgu_ref, wd_ref,
    ctx_ref, out_ref,
    q_all, keys_all, values_near, values_far, relay, scores, softs, ctx_own, ctx_all, wo_all, w_all, res, gains,
    proj, proj_in, hid, scaled, acc, act, down, x_in, x_sum, rings, odd_sum, odd_in,
    send_sem, recv_sem, local_sem,
):
    head = lax.axis_index("head")
    y_lo = lax.axis_index("inner")
    outer = lax.axis_index("outer")
    x, c = head // 2, head % 2
    u, pair, mirror = x % 2, x + 1 - 2 * (x % 2), 3 - x
    y_hi, z = outer // NZ, outer % NZ
    y = y_hi * 4 + y_lo
    other = 1 - c

    def to_head(h):
        return {"head": h}

    def to_x(i):
        return {"head": i * 2 + c}

    def to_y(i):
        return {"inner": i % 4, "outer": (i // 4) * NZ + z}

    def to_z(i):
        return {"outer": y_hi * NZ + i}

    def to_outer(i):
        return {"outer": i}

    def to_lo(i):
        return {"inner": i}

    def to_cross(i):
        return {"head": x * 2 + other, "inner": i}

    sibling = to_head(x * 2 + other)

    def feat(i):
        return (i % 4) * 2 + i // 4

    counter = [0]

    def new(count=1):
        counter[0] += count
        return counter[0] - count

    def remote(src, dst, sid, dev, ssid=0):
        return pltpu.make_async_remote_copy(
            src_ref=src, dst_ref=dst, send_sem=send_sem.at[ssid], recv_sem=recv_sem.at[sid],
            device_id=dev, device_id_type=MESH,
        )

    sent = [0]

    def count(units):
        sent[-1] += units
        if sent[-1] >= FULL and block_shape(sent[-1]) is not None:
            sent.append(0)

    def push(src, dst, sid, dev):
        remote(src, dst, sid, dev, len(sent) - 1).start()
        count(math.prod(src.shape) * jnp.dtype(src.dtype).itemsize // 4096)

    maybes = []

    def push_if(cond, src, dst, sid, dev):
        copy = (src, dst, sid, dev, SHARED + 1 + len(maybes))

        @pl.when(cond)
        def _():
            remote(*copy).start()

        maybes.append((cond, copy))

    def arrive_if(cond, *args):
        @pl.when(cond)
        def _():
            arrive(*args)

    def arrive(dst, sid):
        remote(dst, dst, sid, sibling).wait_recv()

    local_count = [0]

    def local(src, dst, sem=None):
        if sem is None:
            sem = local_sem.at[local_count[0]]
            local_count[0] += 1
        copy = pltpu.make_async_copy(src, dst, sem)
        copy.start()
        return copy

    def ring(n, me, to, chunk, half, arrived=None):
        steps = n // 2
        sr, sl = new(steps), new(steps)
        right, left = to((me + 1) % n), to((me + n - 1) % n)

        def run():
            for s in range(steps):
                back, ahead = (me - s + n) % n, (me + s) % n
                if s > 0:
                    arrive(chunk(back), sr + s - 1)
                    arrive(chunk(ahead), sl + s - 1)
                if s < steps - 1:
                    push(chunk(back), chunk(back), sr + s, right)
                    push(chunk(ahead), chunk(ahead), sl + s, left)
                elif half is None:
                    push(chunk(ahead), chunk(ahead), sl + s, left)
                else:
                    push(half(back, 0), half(back, 0), sr + s, right)
                    push(half(ahead, 1), half(ahead, 1), sl + s, left)
                if arrived is not None:
                    arrived(back, 2 * s)
                    if s > 0:
                        arrived(ahead, 2 * s - 1)
                yield
            far = (me + steps) % n
            if half is None:
                arrive(chunk(far), sl + steps - 1)
            else:
                arrive(half(far, 0), sr + steps - 1)
                arrive(half(far, 1), sl + steps - 1)
            if arrived is not None:
                arrived(far, 2 * steps - 1)

        return run()

    def finish(gen):
        for _ in gen:
            pass

    def together(gens):
        for _ in range(5):
            for gen in gens:
                next(gen, None)

    def lanes(core, width):
        return pl.ds(pl.multiple_of(core * width, width), width)

    keys_all[...] = jnp.zeros_like(keys_all)
    values_near[...] = jnp.zeros_like(values_near)

    barrier = pltpu.get_barrier_semaphore()
    for k in range(1, 8):
        pl.semaphore_signal(barrier, inc=1, device_id=to_head((head + k) % 8), device_id_type=MESH)
        pl.semaphore_signal(barrier, inc=1, device_id=to_y((y + k) % NY), device_id_type=MESH)
    for k in range(1, BACK):
        for peer in ((outer + k) % 16, (outer + 16 - k) % 16):
            pl.semaphore_signal(barrier, inc=1, device_id=to_outer(peer), device_id_type=MESH)
        pl.semaphore_signal(barrier, inc=1, device_id=to_z((z + k) % NZ), device_id_type=MESH)
        pl.semaphore_signal(barrier, inc=1, device_id=to_z((z + NZ - k) % NZ), device_id_type=MESH)
    for k in range(1, 4):
        pl.semaphore_signal(barrier, inc=1, device_id=to_cross((y_lo + k) % 4), device_id_type=MESH)
    pl.semaphore_wait(barrier, 33)

    k_sid, v_sid, q_sid = new(), new(), new()
    for k in range(1, 8):
        peer = (head + k) % 8
        cols = pl.ds(pl.multiple_of(peer * 128, 128), 128)
        push(k_ref.at[:, cols], keys_all.at[0, y_lo, head], k_sid, to_head(peer))
        push(v_ref.at[:, cols], values_near.at[y, head], v_sid, to_head(peer))
    own = pl.ds(pl.multiple_of(head * 128, 128), 128)
    local(k_ref.at[:, own], keys_all.at[0, y_lo, head], recv_sem.at[k_sid])
    local(v_ref.at[:, own], values_near.at[y, head], recv_sem.at[v_sid])
    for k in range(1, 8):
        peer = (head + k) % 8
        cols = pl.ds(pl.multiple_of(peer * 512, 512), 512)
        push(q_ref.at[:, cols], q_all.at[head], q_sid, to_head(peer))
    local(q_ref.at[:, pl.ds(pl.multiple_of(head * 512, 512), 512)], q_all.at[head], recv_sem.at[q_sid])

    w_sid = new()

    def w_cols(part, s):
        return pl.ds(pl.multiple_of(s * 768 + part * 128, 128), 128)

    def w_sources(i):
        cols = pl.ds(pl.multiple_of(i * 128, 128), 128)
        return wgu_ref.at[0, :, cols], wgu_ref.at[1, :, cols], wd_ref.at[:, cols]

    def w_exchange(parts):
        for k in range(1, NY):
            peer = (y + k) % NY

            @pl.when(peer != NY - 1)
            def _(k=k, peer=peer):
                for part in parts:
                    remote(
                        w_sources(peer)[part], w_all.at[feat(y), z, :, w_cols(part, c)],
                        w_sid, to_y(peer), SHARED,
                    ).start()

    def w_exchanged():
        @pl.when(y != NY - 1)
        def _():
            arrive(w_part(z, c, 0, 384), w_sid)

    @pl.when(y != NY - 1)
    def _():
        for part, src in enumerate(w_sources(y)):
            pltpu.make_async_copy(
                src, w_all.at[feat(y), z, :, w_cols(part, c)], recv_sem.at[w_sid]
            ).start()

    @pl.when(y == NY - 1)
    def _():
        def zero(f, _):
            w_all[f, z, :, pl.ds(pl.multiple_of(c * 768, 128), 384)] = jnp.zeros((64, 384), BF)
            return 0

        lax.fori_loop(0, 8, zero, 0)

    wo_sid = new()
    push(wo_ref, wo_all.at[y_hi, z, :, lanes(c, 512)], wo_sid, to_y((1 - y_hi) * 4 + y_lo))
    wo_copy = local(wo_ref, wo_all.at[y_hi, z, :, lanes(c, 512)])
    res_copy = local(resid_ref.at[pl.ds(pl.multiple_of(head * 64, 64), 64)], res)

    arrive(keys_all.at[0, y_lo], k_sid)
    arrive(values_near.at[y], v_sid)

    def shared_ring(buf_chunk, sid, then=None, buf_half=None):
        def arrived(i, n):
            push(buf_chunk(i, c), buf_chunk(i, c), sid, sibling)
            if then is not None:
                then(i, n)

        half = None if buf_half is None else lambda i, b: buf_half(i, b, c)
        return ring(NZ, z, to_z, lambda i: buf_chunk(i, c), half, arrived)

    wo_core_sid = new()
    wo_ring = shared_ring(lambda i, s: wo_all.at[:, i, :, lanes(s, 512)], wo_core_sid)

    ahead_sid, key_sid, near_sid, far_sid = new(BACK), new(4 * BACK), new(8), new(BACK + 1)

    def key_wanted(dz, src, dst):
        seen = outer >= dz
        return seen & (src < dst) if dz == 0 else seen & (src > dst) if dz == 4 else seen

    def key_lo(dz):
        for k in range(1, 4):
            peer = (y_lo + k) % 4
            push_if(
                key_wanted(dz, y_lo, peer),
                keys_all.at[dz, y_lo], keys_all.at[dz, y_lo], key_sid + 4 * dz + k, to_lo(peer),
            )

    def key_ahead(dz):
        arrive_if(outer >= dz, keys_all.at[dz, y_lo], ahead_sid + dz)

    def near_wanted(row):
        return (row == y_hi) | ((z >= 4) & (row == 0))

    for k in range(1, NY):
        peer = (y + k) % NY
        push_if(
            (peer // 4 == y_hi) | ((z >= 4) & (y_hi == 0)),
            values_near.at[y], values_near.at[y], near_sid + k, to_y(peer),
        )
    for dz in range(1, BACK):
        push_if(
            outer + dz < 16,
            keys_all.at[0, y_lo], keys_all.at[dz, y_lo], ahead_sid + dz, to_outer((outer + dz) % 16),
        )
    key_lo(0)
    wo_copy.wait()
    arrive(wo_all.at[1 - y_hi, z, :, lanes(c, 512)], wo_sid)
    next(wo_ring)
    for k in range(1, NY):
        peer = (y + NY - k) % NY
        arrive_if(near_wanted(peer // 4), values_near.at[peer], near_sid + k)
        if k == 4:
            next(wo_ring)

    def row_blocks(dz):
        return values_near.at[pl.ds(jnp.where(z + dz < NZ, y_hi, 1 - y_hi) * 4, 4)]

    push(row_blocks(4), relay, far_sid, to_z((z + NZ - 2) % NZ))
    for dz in range(1, 3):
        push(row_blocks(dz), values_far.at[dz - 1], far_sid + dz, to_z((z + dz) % NZ))
    push_if(z == NZ - 3, row_blocks(3), values_far.at[2], far_sid + 3, to_z((z + 3) % NZ))
    w_exchange([0, 1, 2])
    for dz in range(1, 3):
        key_ahead(dz)
        key_lo(dz)
    next(wo_ring)
    arrive(values_far.at[1], far_sid + 2)
    push_if(z != NZ - 1, values_far.at[1], values_far.at[2], far_sid + 3, to_z((z + 1) % NZ))
    arrive(relay, far_sid)
    push(relay, values_far.at[3], far_sid + 4, to_z((z + NZ - 2) % NZ))
    for dz in range(3, BACK):
        key_ahead(dz)
        key_lo(dz)

    def w_part(i, s, first, width, f=0, count=8):
        return w_all.at[pl.ds(f, count), i, :, pl.ds(pl.multiple_of(s * 768 + first, 128), width)]

    over_sid, mirror_sid, w_core_sid = new(2), new(24), new(4)
    to_mirror = to_x(mirror)
    w_exchanged()
    push(w_part(z, c, 256, 128), w_part(z, c, 384, 128), over_sid, to_mirror)
    push(w_part(z, c, 0, 256, 6, 2), w_part(z, c, 512, 256, 6, 2), over_sid + 1, to_mirror)

    def w_quarter_ring(p):
        if p == 3:
            return shared_ring(
                lambda i, s: w_part(i, s, 0, 768, 6, 2), w_core_sid + 3, None,
                lambda i, b, s: w_part(i, s, 0, 768, 6 + b, 1),
            )

        def w_arrived(i, n):
            push(
                w_part(i, c, 0, 256, 2 * p, 2), w_part(i, c, 512, 256, 2 * p, 2),
                mirror_sid + 8 * p + n, to_mirror,
            )

        return shared_ring(
            lambda i, s: w_part(i, s, 0, 512, 2 * p, 2), w_core_sid + p, w_arrived,
            lambda i, b, s: w_part(i, s, 0, 512, 2 * p + b, 1),
        )

    w_rings = [w_quarter_ring(p) for p in range(4)]

    def w_place(n):
        step = (n + 1) // 2
        return (z + step) % NZ if n % 2 else (z - step + NZ) % NZ

    def w_step(p, *which):
        next(w_rings[p], None)
        for n in which if p < 3 else ():
            gate_up_part = w_part(w_place(n), c, 512, 256, 2 * p, 2)
            arrive(gate_up_part, mirror_sid + 8 * p + n)
            push(gate_up_part, gate_up_part, w_core_sid + p, sibling)

    next(wo_ring)
    gain_sid = new(4)
    for k in range(1, 4):
        push(gain_ref, gains.at[y_lo], gain_sid + k, to_lo((y_lo + k) % 4))
    gains[y_lo] = gain_ref[...]
    arrive(w_part(z, c, 384, 128), over_sid)
    arrive(w_part(z, c, 512, 256, 6, 2), over_sid + 1)
    for p in range(4):
        w_step(p)

    for dz in range(BACK):
        for k in range(1, 4):
            peer = (y_lo + 4 - k) % 4
            arrive_if(key_wanted(dz, peer, y_lo), keys_all.at[dz, peer], key_sid + 4 * dz + k)

    arrive(q_all, q_sid)
    place = outer * 512 + y_lo * 128 + lax.broadcasted_iota(jnp.int32, (128, 1), 0)
    start = jnp.zeros((128, 1), jnp.int32)
    bound = jnp.int32(0)
    for j in range(DOCS):
        bound = bound + docs_ref[j]
        start = jnp.where(bound <= place, bound, start)
    for dz in range(BACK):
        keys = keys_all[dz].reshape(512, 128)
        key_place = (outer - dz) * 512 + lax.broadcasted_iota(jnp.int32, (1, 512), 1)
        bias = jnp.where((key_place <= place) & (key_place >= start), 0.0, -1e30)
        for g in range(4):
            heads_q = q_all[:, :, g * 128:(g + 1) * 128].reshape(128, 128)
            scores[g, :, dz * 512:(dz + 1) * 512] = nt(heads_q, keys) * SCALE + bias
    totals = []
    for g in range(4):
        s = scores[g]
        e = jnp.exp(s - jnp.max(s, axis=1, keepdims=True))
        totals.append(jnp.sum(e, axis=1, keepdims=True))
        softs[g] = e.astype(BF)

    for dz in (1, 3, 4):
        arrive(values_far.at[dz - 1], far_sid + dz)
    for g in range(4):
        summed = jnp.zeros((128, 128), F32)
        for dz in range(BACK):
            values = (values_near[pl.ds(y_hi * 4, 4)] if dz == 0 else values_far[dz - 1]).reshape(512, 128)
            summed += jnp.dot(softs[g, :, dz * 512:(dz + 1) * 512], values, preferred_element_type=F32)
        ctx_own[:, g * 128:(g + 1) * 128] = (summed / totals[g]).astype(BF)

    def half_rows(i):
        return ctx_own.at[pl.ds(pl.multiple_of(i * 64, 64), 64)]

    ctx_copy = local(ctx_own, ctx_ref)

    def ctx_part(i, core):
        return ctx_all.at[i, :, lanes(core, 512)]

    ctx_sid, cross_sid = new(4), new(4)
    for k in range(1, 4):
        peer = (y_lo + k) % 4
        push(half_rows(c), ctx_part(y_lo, c), ctx_sid + k, to_lo(peer))
        push(half_rows(other), ctx_part(y_lo, c), cross_sid + k, to_cross(peer))
    push(half_rows(other), ctx_part(y_lo, c), cross_sid, sibling)
    ctx_all[y_lo, :, lanes(c, 512)] = half_rows(c)[...]

    w_step(0, 0)
    w_step(1, 0)

    proj_sid = new(4)

    def proj_push(i):
        way = (i + NX - x) % NX
        return remote(proj.at[i], proj_in.at[way], proj_sid + way, to_x(i), PROJ)

    finish(wo_ring)
    arrive(wo_all.at[:, :, :, lanes(other, 512)], wo_core_sid)
    for k in range(4):
        i = (y_lo + 4 - k) % 4
        if k > 0:
            arrive(ctx_part(i, c), ctx_sid + k)
        arrive(ctx_part(i, other), cross_sid + k)
        proj[i] = nt(ctx_all[i], wo_all[...].reshape(1024, 1024)).astype(BF)

        @pl.when(i != x)
        def _(i=i):
            proj_push(i).start()

        if k in (1, 2):
            w_step(k + 1, 0)

    res_copy.wait()
    total = proj[x].astype(F32)
    for k in range(1, NX):
        arrive(proj_in.at[k], proj_sid + k)
        total += proj_in[k].astype(F32)
    total = (res[...].astype(F32) + total).astype(BF)
    for b in range(2):
        hid[y_lo, b, y_hi, u] = total[:, b * 512:(b + 1) * 512]
    def hid_part(i, b, p, half=None):
        part = hid.at[i % 4, b, i // 4, p]
        return part if half is None else part.at[pl.ds(half * 32, 32)]

    first_sid, second_sid = new(), new()
    to_pair = to_x(pair)

    def along_x(i, n):
        push(hid_part(i, 1, u), hid_part(i, 1, u), second_sid, to_pair)

    push(hid_part(y, 0, u), hid_part(y, 0, u), first_sid, to_pair)
    y_first = ring(
        NY, y, to_y, lambda i: hid_part(i, 1, u),
        lambda i, b: hid_part(i, 1, u, b), along_x,
    )
    next(y_first)
    w_step(0, 1, 2)
    w_step(1, 1, 2)
    arrive(hid_part(y, 0, 1 - u), first_sid)
    x_first = [
        ring(
            NY, y, to_y, lambda i, p=p: hid_part(i, 0, p),
            lambda i, b, p=p: hid_part(i, 0, p, b),
        )
        for p in range(2)
    ]
    for s in range(4):
        next(x_first[0])
        next(x_first[1])
        next(y_first, None)
        if s == 0:
            w_step(2, 1, 2)
            w_step(3, 1, 2)
        if s in (1, 2):
            w_step(2 * s - 2, 3, 4)
            w_step(2 * s - 1, 3, 4)
        if s == 3:
            w_step(0)
            w_step(1)
    for gen in x_first:
        next(gen, None)
    arrive(hid.at[:, 1, :, 1 - u], second_sid)
    for k in range(1, 4):
        arrive(gains.at[(y_lo + 4 - k) % 4], gain_sid + k)
    w_step(2)
    w_step(3)
    for p in range(3):
        w_step(p, 5, 6)
    acc[...] = jnp.zeros_like(acc)

    def scale(f, squares):
        gain_row = gains[f // 2]
        rows = hid[f // 2, f % 2].reshape(256, 512).astype(F32)
        scaled[f] = jnp.concatenate(
            [
                rows[:, j * 128:(j + 1) * 128]
                * jnp.where(f % 2 == 0, gain_row[j:j + 1], gain_row[4 + j:5 + j])
                for j in range(4)
            ],
            axis=1,
        ).astype(BF)
        return squares + jnp.sum(rows * rows, axis=1, keepdims=True)

    squares = lax.fori_loop(0, 8, scale, jnp.zeros((256, 1), F32))

    def gate_up(f, _):
        for s, first in enumerate(SLOTS):
            weights = w_all[f, :, :, first:first + 256].reshape(512, 256)
            acc[s] += jnp.dot(scaled[f], weights, preferred_element_type=F32)
        return 0

    for p in (3, 0, 1, 2):
        w_step(p, 7)
        arrive(w_all.at[pl.ds(2 * p, 2), :, :, lanes(other, 768)], w_core_sid + p)
    lax.fori_loop(0, 8, gate_up, 0)

    inverse = lax.rsqrt(squares / D + 1e-05)
    for s in range(4):
        gate, up = acc[s, :, :128] * inverse, acc[s, :, 128:] * inverse
        act[:, s * 128:(s + 1) * 128] = (gate / (1.0 + jnp.exp(-gate)) * up).astype(BF)

    x_sid, odd_sid = new(4), new()

    def project_down(lo, b):
        f = lo * 2 + b
        weights = jnp.concatenate(
            [w_all[f, :, :, s * 768 + 256:s * 768 + 512].reshape(512, 256) for s in range(2)], axis=1
        )
        down[lo, b] = nt(act[...], weights).astype(BF).reshape(2, 2, 64, 512)

    def sum_ring(block, slots):
        sid = new(8)
        to_way = to_y((y + 1) % NY), to_y((y + NY - 1) % NY)

        def run():
            for s in range(4):
                for way in range(2):
                    buf, first_sid = slots.at[way], sid + 4 * way
                    i = (y + 4 - s) % NY if way == 0 else (y + 4 + s) % NY
                    half = pl.ds(32 * way, 32)
                    if s == 0:
                        push(block(i, 32 * way, 32), buf.at[0, half], first_sid, to_way[way])
                        continue
                    if s == 1:
                        arrive(buf.at[0, half], first_sid)
                        mine = block(i, 32 * way, 32)[...]
                        buf[0, half] = (buf[0, half].astype(F32) + mine.astype(F32)).astype(BF)
                        buf[0, pl.ds(32 * (1 - way), 32)] = block(i, 32 * (1 - way), 32)[...]
                    else:
                        arrive(buf.at[s - 1], first_sid + s - 1)
                        mine = block(i, 0, 64)[...]
                        buf[s - 1] = (buf[s - 1].astype(F32) + mine.astype(F32)).astype(BF)
                    push(buf.at[s - 1], buf.at[s], first_sid + s, to_way[way])
                yield

        def total():
            result = block(y, 0, 64)[...].astype(F32)
            for way in range(2):
                arrive(slots.at[way, 3], sid + 4 * way + 3)
                result += slots[way, 3].astype(F32)
            return result

        return run(), total

    odd_rings = [
        sum_ring(
            lambda i, first, count, p=p: down.at[i % 4, 1, i // 4, p, pl.ds(first, count)], rings.at[p]
        )
        for p in range(2)
    ]
    even_ring = sum_ring(lambda i, first, count: x_sum.at[i % 4, i // 4, pl.ds(first, count)], rings.at[2])

    def odd_step():
        for gen, _ in odd_rings:
            next(gen)

    def add_even(*pieces):
        for k in pieces:
            lo = (y_lo + k) % 4
            arrive(x_in.at[k], x_sid + k)
            for g in range(2):
                x_sum[lo, g] = (down[lo, 0, g, u].astype(F32) + x_in[k, g].astype(F32)).astype(BF)
        next(even_ring[0])

    for k in (0, 1, 3, 2):
        lo = (y_lo + k) % 4
        project_down(lo, 0)
        push(down.at[lo, 0, :, 1 - u], x_in.at[k], x_sid + k, to_pair)
    for k in (0, 1, 3, 2):
        project_down((y_lo + k) % 4, 1)
        if k == 0:
            odd_step()

    add_even(0)
    odd_step()
    add_even(1, 3)
    odd_step()
    add_even(2)
    odd_step()
    add_even()
    for p in range(2):
        odd_sum[p] = odd_rings[p][1]().astype(BF)
    push(odd_sum.at[1 - u], odd_in, odd_sid, to_pair)
    out_ref[:, :512] = (hid[y_lo, 0, y_hi, u].astype(F32) + even_ring[1]()).astype(BF)
    arrive(odd_in, odd_sid)
    total = odd_sum[u].astype(F32) + odd_in[...].astype(F32)
    out_ref[:, 512:] = (hid[y_lo, 1, y_hi, u].astype(F32) + total).astype(BF)

    ctx_copy.wait()
    if sent[-1] == 0:
        sent.pop()
    for ssid, units in enumerate(sent):
        block = w_all.at[tuple(pl.ds(0, n) for n in block_shape(units))]
        remote(block, block, 0, sibling, ssid).wait_send()
    for cond, copy in maybes:
        @pl.when(cond)
        def _(copy=copy):
            remote(*copy).wait_send()

    remote(proj.at[pl.ds(0, 3)], proj.at[pl.ds(0, 3)], 0, sibling, PROJ).wait_send()

    for last, count in ((False, 6), (True, 7)):
        @pl.when((y == NY - 1) == last)
        def _(count=count):
            pieces = w_all.at[pl.ds(0, count), 0, :, pl.ds(0, 384)]
            remote(pieces, pieces, 0, sibling, SHARED).wait_send()

    assert counter[0] == RECV and len(sent) == SHARED and local_count[0] == LOCAL, (counter[0], len(sent), sent)
    assert PROJ + 1 == SEND and len(maybes) == MAYBES, len(maybes)


RECV, LOCAL, MAYBES, SHARED, FULL = 186, 3, 28, 18, 244
PROJ = SHARED + 1 + MAYBES
SEND = PROJ + 1


def block_shape(units):
    shapes = (
        (a, b, 16 * r, 128 * t)
        for a in range(1, 9) for b in range(1, 9) for r in range(1, 5) for t in range(1, 13)
        if a * b * r * t == units
    )
    return next(shapes, None)


SLOTS = (0, 512, 768, 1280)


def per_device(query, key, value, doc_lengths, resid, norm_gain, w_out, w_gate_up, w_down):
    vmem = pl.BlockSpec(memory_space=pltpu.VMEM)
    anywhere = pl.BlockSpec(memory_space=pl.ANY)
    smem = pl.BlockSpec(memory_space=pltpu.SMEM)

    def buf(*shape, kind=BF):
        return pltpu.VMEM(shape, kind)

    return pl.pallas_call(
        kernel,
        out_shape=(
            jax.ShapeDtypeStruct((128, 512), BF),
            jax.ShapeDtypeStruct((64, 1024), BF),
        ),
        in_specs=[anywhere, anywhere, anywhere, smem, anywhere, vmem, anywhere, anywhere, anywhere],
        out_specs=(anywhere, vmem),
        scratch_shapes=[
            buf(8, 16, 512),
            buf(BACK, 4, 8, 16, 128),
            buf(8, 8, 16, 128),
            buf(BACK - 1, 4, 8, 16, 128),
            buf(4, 8, 16, 128),
            buf(4, 128, BACK * 512, kind=F32),
            buf(4, 128, BACK * 512),
            buf(128, 512),
            buf(4, 64, 1024),
            buf(2, 8, 64, 1024),
            buf(8, 8, 64, 1536),
            buf(64, 1024),
            buf(4, 8, 128, kind=F32),
            buf(4, 64, 1024),
            buf(4, 64, 1024),
            buf(4, 2, 2, 2, 64, 512),
            buf(8, 256, 512),
            buf(4, 256, 256, kind=F32),
            buf(256, 512),
            buf(4, 2, 2, 2, 64, 512),
            buf(4, 2, 64, 512),
            buf(4, 2, 64, 512),
            buf(3, 2, 4, 64, 512),
            buf(2, 64, 512),
            buf(64, 512),
            pltpu.SemaphoreType.DMA((SEND,)),
            pltpu.SemaphoreType.DMA((RECV,)),
            pltpu.SemaphoreType.DMA((LOCAL,)),
        ],
        compiler_params=pltpu.CompilerParams(
            collective_id=0, has_side_effects=True, vmem_limit_bytes=56 * 1024 * 1024
        ),
        cost_estimate=pl.CostEstimate(flops=4_000_000_000, bytes_accessed=4_000_000, transcendentals=2_000_000),
    )(
        query, key, value, doc_lengths, resid, norm_gain.reshape(8, 128),
        w_out.T, w_gate_up, w_down.T,
    )


def solution(mesh):
    placed = (
        P(("outer", "inner", "head"), None),
        P(("outer", "inner", "head"), None),
        P(("outer", "inner", "head"), None),
        P(),
        P("outer", "inner"),
        P("inner"),
        P("head", ("inner", "outer")),
        P(None, ("inner", "outer"), "head"),
        P("head", ("inner", "outer")),
    )
    return jax.shard_map(
        per_device,
        mesh=mesh,
        in_specs=placed,
        out_specs=(P(("outer", "inner"), "head"), P(("outer", "head"), "inner")),
        check_vma=False,
    )
```
